32 devices in a mesh: dp: 16 (over z, y, core), mp: 2 (over x).
Axes of the slice: x: 2, y: 2, z: 4, core: 2. Of those that a mesh axis runs over, the one named last changes fastest.
Arguments:
- image_pooled: bfloat16 [2048, 1152], P('dp'), may hold values from -6 to 6
- text_last: bfloat16 [2048, 1152], P('dp'), may hold values from -6 to 6
- caption_of: int32 [2048], P('dp'), may hold values from 0 to 2047
- image_gain: float32 [1152], replicated, may hold values from 0.1 to 1.9
- text_gain: float32 [1152], replicated, may hold values from 0.1 to 1.9
- mlp_up: bfloat16 [1152, 4304], P(None, 'mp'), may hold values from -0.1875 to 0.1875
- mlp_down: bfloat16 [4304, 1152], P('mp'), may hold values from -0.09375 to 0.09375
- adapter: bfloat16 [1152, 1152], P('mp'), may hold values from -0.0029296875 to 0.0029296875
- logit_scale: float32 [1], replicated, may hold values from 30 to 100
- logit_bias: float32 [1], replicated, may hold values from -4 to -1
Outputs:
- grad_adapter: bfloat16 [1152, 1152], P('mp')
- mean_loss: float32 [1], replicated
The draws below stay inside these ranges and needn't reach their ends.
Inputs may be any that keep to these rules, and one draw needn't show every extreme that they name: caption_of[j] is the index of the image that text j describes.
All inputs are finite; a program needn't handle non-finite values.
Results may differ from the reference program's by a relative error of at most 0.00175.
The reference program's roundings to bfloat16 on the way (of `image_norm`, `hidden`, `image_unit`, `text_norm`, `text_embed` and `pair_weight`) count: a program that leaves them out, or rounds other values in their place, can miss the bound.
Values may be sent and summed in bfloat16 or wider, within the bound.
No kernel may reach another device: no remote copies, remote signals or barrier semaphores. Data moves between devices by JAX's collectives and lax.ppermute only.
A program may use at most 128 MiB of HBM per device.

```python
import math
import jax
import jax.numpy as jnp
from jax import lax

D = 1152
FF = 4304
PAIRS = 2048


def plant(drawn, stream_key, low, top_value):
    shape = drawn.shape
    index_at = [jax.random.randint(jax.random.fold_in(stream_key, axis), (), 0, shape[axis]) for axis in range(len(shape))]
    drawn = drawn.at[tuple(index_at)].set(low)
    longest = shape.index(max(shape))
    index_at[longest] = (index_at[longest] + 1) % shape[longest]
    return drawn.at[tuple(index_at)].set(top_value)


def block_scale(stream_key, extent, shards, least, high):
    level, own = 1.0, jax.random.fold_in(stream_key, 6)
    for axis_at, shards_of in shards:
        steps = jnp.exp(jax.random.uniform(jax.random.fold_in(own, axis_at), (shards_of,), jnp.float32, least / len(shards), high / len(shards)))
        level = level * jnp.repeat(steps, extent[axis_at] // shards_of).reshape([-1 if axis == axis_at else 1 for axis in range(len(extent))])
    return level


def noise(stream_key, shape, scale, reach, split=(), kind=jnp.bfloat16):
    values = jax.random.normal(stream_key, shape, jnp.float32) * scale
    if len(split) > 0:
        values = block_scale(stream_key, shape, split, -0.22, 0.18) * values
    return jnp.clip(values, min=-reach, max=reach).astype(kind)


def setup_inputs(seed: int = 0) -> dict:
    key_list = jax.random.split(jax.random.key(seed), 11)
    return {
        "image_pooled": noise(key_list[0], (PAIRS, D), 1.0, 6.0, ((0, 16),)),
        "text_last": noise(key_list[1], (PAIRS, D), 1.0, 6.0, ((0, 16),)),
        "caption_of": plant(jax.random.randint(key_list[2], (PAIRS,), 0, PAIRS), jax.random.fold_in(key_list[2], 1), 0, PAIRS - 1).astype(jnp.int32),
        "image_gain": jnp.clip(1.0 + 0.18 * jax.random.normal(key_list[3], (D,), jnp.float32), 0.1, 1.9),
        "text_gain": jnp.clip(1.0 + 0.18 * jax.random.normal(key_list[4], (D,), jnp.float32), 0.1, 1.9),
        "mlp_up": noise(key_list[5], (D, FF), D ** -0.5, 0.1875, ((1, 2),)),
        "mlp_down": noise(key_list[6], (FF, D), FF ** -0.5, 0.09375, ((0, 2),)),
        "adapter": noise(key_list[7], (D, D), (4096 * D) ** -0.5, 0.0029296875, ((0, 2),)),
        "logit_scale": jnp.clip(jnp.exp(jax.random.uniform(key_list[8], (1,), jnp.float32, math.log(30.0), math.log(100.0))), 30.0, 100.0),
        "logit_bias": jnp.clip(jax.random.uniform(key_list[9], (1,), jnp.float32, -4.0, -1.0), -4.0, -1.0),
    }


EPS = 1e-06

def layer_norm(values, gain):
    values = values.astype(jnp.float32)
    center = values - lax.optimization_barrier(jnp.mean(values, axis=-1, keepdims=True))
    spread = lax.optimization_barrier(jnp.mean(center * center, axis=-1, keepdims=True))
    return center * lax.rsqrt(spread + EPS) * gain

def reference(image_pooled, text_last, caption_of, image_gain, text_gain, mlp_up, mlp_down, adapter, logit_scale, logit_bias):
    image_norm = layer_norm(image_pooled, image_gain).astype(jnp.bfloat16)
    hidden = jax.nn.gelu(jnp.dot(image_norm, mlp_up, preferred_element_type=jnp.float32), approximate=True).astype(jnp.bfloat16)
    feature = image_pooled.astype(jnp.float32) + jnp.dot(hidden, mlp_down, preferred_element_type=jnp.float32)
    image_unit = (feature * lax.rsqrt(lax.optimization_barrier(jnp.sum(feature * feature, axis=-1, keepdims=True)) + EPS)).astype(jnp.bfloat16)
    text_norm = layer_norm(text_last, text_gain).astype(jnp.bfloat16)
    texts = jnp.dot(text_norm, adapter, preferred_element_type=jnp.float32)
    inverse = lax.rsqrt(lax.optimization_barrier(jnp.sum(texts * texts, axis=-1, keepdims=True)) + EPS)
    text_unit = texts * inverse
    text_embed = text_unit.astype(jnp.bfloat16)
    scale = logit_scale[0]
    shift = logit_bias[0]
    block = math.gcd(PAIRS, 512)
    image_index = jnp.arange(PAIRS, dtype=jnp.int32)

    def one_block(number):
        begin = (number * block).astype(jnp.int32)
        rows_embed = lax.dynamic_slice_in_dim(text_embed, begin, block, 0)
        rows_caption = lax.dynamic_slice_in_dim(caption_of, begin, block, 0)
        logits = lax.dot_general(rows_embed, image_unit, (((1,), (1,)), ((), ())), preferred_element_type=jnp.float32)
        labels = jnp.where(rows_caption[:, None] == image_index[None, :], 1.0, -1.0).astype(jnp.float32)
        scores = scale * logits + shift
        loss_sum = jnp.sum(jax.nn.softplus(-labels * scores))
        pair_weight = (-labels * jax.nn.sigmoid(-labels * scores)).astype(jnp.bfloat16)
        grads = jnp.dot(pair_weight, image_unit, preferred_element_type=jnp.float32)
        return (loss_sum, grads)
    losses, grads = lax.map(one_block, jnp.arange(PAIRS // block, dtype=jnp.int32))
    grads = grads.reshape(PAIRS, D)
    scaled = grads * (scale / PAIRS)
    along = lax.optimization_barrier(jnp.sum(text_unit * scaled, axis=-1, keepdims=True))
    resid = (scaled - text_unit * along) * inverse
    grad_adapter = jnp.dot(text_norm.astype(jnp.float32).T, resid, precision=lax.Precision.HIGHEST, preferred_element_type=jnp.float32).astype(jnp.bfloat16)
    mean_loss = (jnp.sum(losses) / (PAIRS * PAIRS)).reshape(1)
    return (grad_adapter, mean_loss)
```

```python
import jax
import jax.numpy as jnp
from jax import lax
from jax.sharding import PartitionSpec as P

EPS = 1e-06
CORE, Y, Z_LOW, Z_HIGH = 1, 2, 4, 8


def layer_norm(values, gain):
    values = values.astype(jnp.float32)
    center = values - jnp.mean(values, axis=-1, keepdims=True)
    spread = jnp.mean(center * center, axis=-1, keepdims=True)
    return center * lax.rsqrt(spread + EPS) * gain


def text_resid(grads, text_unit, inverse, factor):
    scaled = grads * factor
    along = jnp.sum(text_unit * scaled, axis=-1, keepdims=True)
    return (scaled - text_unit * along) * inverse


def outer_sum(left, right):
    return lax.dot_general(
        left.astype(jnp.float32),
        right,
        (((0,), (0,)), ((), ())),
        precision=lax.Precision.HIGHEST,
        preferred_element_type=jnp.float32,
    )


def general_plan(
    image_pooled,
    text_last,
    caption_of,
    image_gain,
    text_gain,
    mlp_up,
    mlp_down,
    adapter,
    logit_scale,
    logit_bias,
):
    row_count = image_pooled.shape[0]
    mp_count = lax.axis_size("mp")
    mp_index = lax.axis_index("mp")
    dp_count = lax.axis_size("dp")
    half_rows = row_count // mp_count
    pair_count = row_count * dp_count
    image_norm = layer_norm(image_pooled, image_gain).astype(jnp.bfloat16)
    hidden = jax.nn.gelu(
        jnp.dot(image_norm, mlp_up, preferred_element_type=jnp.float32), approximate=True
    ).astype(jnp.bfloat16)
    branch = lax.psum_scatter(
        jnp.dot(hidden, mlp_down, preferred_element_type=jnp.float32),
        "mp",
        scatter_dimension=0,
        tiled=True,
    )
    own_pooled = lax.dynamic_slice_in_dim(image_pooled, mp_index * half_rows, half_rows, 0)
    feature = own_pooled.astype(jnp.float32) + branch
    image_unit = (
        feature * lax.rsqrt(jnp.sum(feature * feature, axis=-1, keepdims=True) + EPS)
    ).astype(jnp.bfloat16)
    text_norm = layer_norm(text_last, text_gain).astype(jnp.bfloat16)
    in_width = adapter.shape[0]
    text_part = lax.dynamic_slice_in_dim(text_norm, mp_index * in_width, in_width, 1)
    texts = lax.psum(jnp.dot(text_part, adapter, preferred_element_type=jnp.float32), "mp")
    inverse = lax.rsqrt(jnp.sum(texts * texts, axis=-1, keepdims=True) + EPS)
    text_unit = texts * inverse
    text_embed = text_unit.astype(jnp.bfloat16)
    scale = logit_scale[0]
    shift = logit_bias[0]
    piece = lax.all_gather(image_unit, "dp", axis=0, tiled=True)
    count = piece.shape[0]
    position = jnp.arange(count, dtype=jnp.int32)
    image_index = position // half_rows * row_count + mp_index * half_rows + position % half_rows
    logits = lax.dot_general(
        text_embed, piece, (((1,), (1,)), ((), ())), preferred_element_type=jnp.float32
    )
    labels = jnp.where(caption_of[:, None] == image_index[None, :], 1.0, -1.0).astype(jnp.float32)
    scores = scale * logits + shift
    loss_sum = jnp.sum(jax.nn.softplus(-labels * scores))
    pair_weight = (-labels * jax.nn.sigmoid(-labels * scores)).astype(jnp.bfloat16)
    grads = jnp.dot(pair_weight, piece, preferred_element_type=jnp.float32)
    grads, loss_sum = (grads, loss_sum)
    factor = scale / pair_count
    full_grads, loss_part = lax.psum((grads, loss_sum.reshape(1)), "mp")
    upper = outer_sum(text_part, text_resid(full_grads, text_unit, inverse, factor))
    grad_total, loss_total = lax.psum((upper, loss_part), "dp")
    mean_loss = loss_total / (pair_count * pair_count)
    return (grad_total.astype(jnp.bfloat16), mean_loss)


def swap(values, axis, bit):
    count = lax.axis_size(axis)
    return lax.ppermute(values, axis, [(i, i ^ bit) for i in range(count)])


def swap_x(values):
    return swap(values, "mp", 1)


def swap_core(values):
    return swap(values, "dp", CORE)


def join(mine, other, upper):
    return jnp.concatenate([jnp.where(upper, other, mine), jnp.where(upper, mine, other)], axis=0)


def bit_of(index, bit):
    return (index & bit) != 0


def dot_f32(left, right, left_axis, right_axis):
    return lax.dot_general(
        left, right, (((left_axis,), (right_axis,)), ((), ())), preferred_element_type=jnp.float32
    )


def half_of(values, upper, half):
    return jnp.where(upper, values[half:], values[:half])


def pair_terms(scores, matched):
    decay = jnp.exp(-jnp.abs(scores))
    loss = jnp.maximum(scores, 0.0) + jnp.log1p(decay) - jnp.where(matched, scores, 0.0)
    ratio = 1.0 / (1.0 + decay)
    above = jnp.where((scores >= 0.0) != matched, ratio, decay * ratio)
    return loss, jnp.where(matched, -above, above)


def slice_plan(
    image_pooled,
    text_last,
    caption_of,
    image_gain,
    text_gain,
    mlp_up,
    mlp_down,
    adapter,
    logit_scale,
    logit_bias,
):
    rows = image_pooled.shape[0]
    half_rows = rows // 2
    quarter = rows // 4
    dp = lax.axis_index("dp")
    mp = lax.axis_index("mp")
    dp_count = lax.axis_size("dp")
    pair_count = rows * dp_count
    own_c, own_y, own_z1, own_z2 = (bit_of(dp, b) for b in (CORE, Y, Z_LOW, Z_HIGH))
    own_x = bit_of(mp, 1)
    upper_of = {Y: own_y, Z_LOW: own_z1, Z_HIGH: own_z2}

    def grow(values, bit):
        return join(values, swap(values, "dp", bit), upper_of[bit])

    text_a, text_b = text_last[:half_rows], text_last[half_rows:]
    for bit_a, bit_b in ((Z_HIGH, Y), (Z_LOW, Z_HIGH), (Y, Z_LOW)):
        text_a = grow(text_a, bit_a)
        text_b = grow(text_b, bit_b)
    texts_raw = jnp.concatenate([text_a, text_b], axis=0)
    captions = lax.all_gather(caption_of, "dp", axis=0, tiled=True).reshape(2, 2, 2, 2, 2, half_rows)
    captions = jnp.where(own_c, captions[:, :, :, 1], captions[:, :, :, 0])
    cap_a = captions[:, :, :, 0].transpose(2, 1, 0, 3).reshape(-1)
    cap_b = captions[:, :, :, 1].transpose(1, 0, 2, 3).reshape(-1)
    caption = jnp.concatenate([cap_a, cap_b])

    in_width = adapter.shape[0]
    in_half = in_width // 2
    piece = swap_x(half_of(adapter, own_c, in_half))
    other_adapter = join(piece, swap_core(piece), own_c)

    image_norm = layer_norm(image_pooled, image_gain).astype(jnp.bfloat16)
    hidden = jax.nn.gelu(
        jnp.dot(image_norm, mlp_up, preferred_element_type=jnp.float32), approximate=True
    ).astype(jnp.bfloat16)
    branch = jnp.dot(hidden, mlp_down, preferred_element_type=jnp.float32)
    arrived = swap_x(half_of(branch, ~own_x, half_rows))
    feature = half_of(image_pooled, own_x, half_rows).astype(jnp.float32) + (
        half_of(branch, own_x, half_rows) + arrived
    )
    image_unit = (
        feature * lax.rsqrt(jnp.sum(feature * feature, axis=-1, keepdims=True) + EPS)
    ).astype(jnp.bfloat16)

    text_norm = layer_norm(texts_raw, text_gain).astype(jnp.bfloat16)
    low, high = text_norm[:, :in_width], text_norm[:, in_width:]
    text_part = jnp.where(own_x, high, low)
    text_rest = jnp.where(own_x, low, high)
    texts = dot_f32(text_part, adapter, 1, 0) + dot_f32(text_rest, other_adapter, 1, 0)
    inverse = lax.rsqrt(jnp.sum(texts * texts, axis=-1, keepdims=True) + EPS)
    text_unit = texts * inverse
    text_embed = text_unit.astype(jnp.bfloat16)
    scale = logit_scale[0]
    shift = logit_bias[0]

    steps = jnp.arange(quarter, dtype=jnp.int32)

    def score(images, index):
        partner = index ^ rows
        images = jnp.concatenate([images, swap_core(images)], axis=0)
        index = jnp.concatenate([index, partner])
        scores = scale * dot_f32(text_embed, images, 1, 1) + shift
        loss, weight = pair_terms(scores, caption[:, None] == index[None, :])
        return jnp.sum(loss), jnp.dot(
            weight.astype(jnp.bfloat16), images, preferred_element_type=jnp.float32
        )

    def grow_index(index, bit, weight):
        low_index = index & ~(bit * weight)
        return jnp.concatenate([low_index, low_index | (bit * weight)])

    base = dp * rows + mp * half_rows + steps
    image_a, index_a = image_unit[:quarter], base
    image_b, index_b = image_unit[quarter:], base + quarter
    image_a = grow(image_a, Z_HIGH)
    image_b = join(image_b, swap_x(image_b), own_x)
    image_a = grow(image_a, Z_LOW)
    image_b = grow(image_b, Z_HIGH)
    image_a = grow(image_a, Y)
    image_b = grow(image_b, Z_LOW)
    for bit in (Z_HIGH, Z_LOW, Y):
        index_a = grow_index(index_a, bit, rows)
    index_b = grow_index(index_b, 1, half_rows)
    for bit in (Z_HIGH, Z_LOW):
        index_b = grow_index(index_b, bit, rows)
    far_a = swap_x(image_a)
    far_b = swap(image_b, "dp", Y)
    loss_a, grads_a = score(image_a, index_a)
    loss_b, grads_b = score(image_b, index_b)
    loss_c, grads_c = score(far_a, index_a ^ half_rows)
    loss_d, grads_d = score(far_b, index_b ^ (Y * rows))
    loss = (loss_a + loss_c) + (loss_b + loss_d)
    grads = (grads_a + grads_c) + (grads_b + grads_d)

    resid = text_resid(grads, text_unit, inverse, scale / pair_count)
    top = lax.reduce_precision(resid, 8, 7)
    rest = (resid - top).astype(jnp.bfloat16)
    top = top.astype(jnp.bfloat16)

    def outer(part):
        return dot_f32(part, top, 0, 0) + dot_f32(part, rest, 0, 0)

    first, second = text_part[:, :in_half], text_part[:, in_half:]
    given = outer(jnp.where(own_c, first, second))
    kept = outer(jnp.where(own_c, second, first))
    total = (kept + swap_core(given)).astype(jnp.bfloat16)
    grad_adapter = join(total, swap_core(total), own_c)
    loss = loss.reshape(1)
    mean_loss = (loss + swap_core(loss)) / (pair_count * pair_count)
    return grad_adapter, mean_loss


def solution(mesh):
    placed = (
        P("dp", None),
        P("dp", None),
        P("dp"),
        P(),
        P(),
        P(None, "mp"),
        P("mp", None),
        P("mp", None),
        P(),
        P(),
    )
    plan = slice_plan if dict(mesh.shape) == {"dp": 16, "mp": 2} else general_plan
    return jax.shard_map(
        plan, mesh=mesh, in_specs=placed, out_specs=(P("mp", None), P()), check_vma=False
    )
```

```python
import jax
import jax.numpy as jnp
import numpy as np
from jax import lax
from jax.sharding import PartitionSpec as P

EPS = 1e-06
CORE, Y, Z_LOW, Z_HIGH = 1, 2, 4, 8


def layer_norm(values, gain):
    values = values.astype(jnp.float32)
    center = values - jnp.mean(values, axis=-1, keepdims=True)
    spread = jnp.mean(center * center, axis=-1, keepdims=True)
    return center * lax.rsqrt(spread + EPS) * gain


def text_resid(grads, text_unit, inverse, factor):
    scaled = grads * factor
    along = jnp.sum(text_unit * scaled, axis=-1, keepdims=True)
    return (scaled - text_unit * along) * inverse


def outer_sum(left, right):
    return lax.dot_general(
        left.astype(jnp.float32),
        right,
        (((0,), (0,)), ((), ())),
        precision=lax.Precision.HIGHEST,
        preferred_element_type=jnp.float32,
    )


def general_plan(
    image_pooled,
    text_last,
    caption_of,
    image_gain,
    text_gain,
    mlp_up,
    mlp_down,
    adapter,
    logit_scale,
    logit_bias,
):
    row_count = image_pooled.shape[0]
    mp_count = lax.axis_size("mp")
    mp_index = lax.axis_index("mp")
    dp_count = lax.axis_size("dp")
    half_rows = row_count // mp_count
    pair_count = row_count * dp_count
    image_norm = layer_norm(image_pooled, image_gain).astype(jnp.bfloat16)
    hidden = jax.nn.gelu(
        jnp.dot(image_norm, mlp_up, preferred_element_type=jnp.float32), approximate=True
    ).astype(jnp.bfloat16)
    branch = lax.psum_scatter(
        jnp.dot(hidden, mlp_down, preferred_element_type=jnp.float32),
        "mp",
        scatter_dimension=0,
        tiled=True,
    )
    own_pooled = lax.dynamic_slice_in_dim(image_pooled, mp_index * half_rows, half_rows, 0)
    feature = own_pooled.astype(jnp.float32) + branch
    image_unit = (
        feature * lax.rsqrt(jnp.sum(feature * feature, axis=-1, keepdims=True) + EPS)
    ).astype(jnp.bfloat16)
    text_norm = layer_norm(text_last, text_gain).astype(jnp.bfloat16)
    in_width = adapter.shape[0]
    text_part = lax.dynamic_slice_in_dim(text_norm, mp_index * in_width, in_width, 1)
    texts = lax.psum(jnp.dot(text_part, adapter, preferred_element_type=jnp.float32), "mp")
    inverse = lax.rsqrt(jnp.sum(texts * texts, axis=-1, keepdims=True) + EPS)
    text_unit = texts * inverse
    text_embed = text_unit.astype(jnp.bfloat16)
    scale = logit_scale[0]
    shift = logit_bias[0]
    piece = lax.all_gather(image_unit, "dp", axis=0, tiled=True)
    count = piece.shape[0]
    position = jnp.arange(count, dtype=jnp.int32)
    image_index = position // half_rows * row_count + mp_index * half_rows + position % half_rows
    logits = lax.dot_general(
        text_embed, piece, (((1,), (1,)), ((), ())), preferred_element_type=jnp.float32
    )
    labels = jnp.where(caption_of[:, None] == image_index[None, :], 1.0, -1.0).astype(jnp.float32)
    scores = scale * logits + shift
    loss_sum = jnp.sum(jax.nn.softplus(-labels * scores))
    pair_weight = (-labels * jax.nn.sigmoid(-labels * scores)).astype(jnp.bfloat16)
    grads = jnp.dot(pair_weight, piece, preferred_element_type=jnp.float32)
    grads, loss_sum = (grads, loss_sum)
    factor = scale / pair_count
    full_grads, loss_part = lax.psum((grads, loss_sum.reshape(1)), "mp")
    upper = outer_sum(text_part, text_resid(full_grads, text_unit, inverse, factor))
    grad_total, loss_total = lax.psum((upper, loss_part), "dp")
    mean_loss = loss_total / (pair_count * pair_count)
    return (grad_total.astype(jnp.bfloat16), mean_loss)


def swap(values, axis, bit):
    count = lax.axis_size(axis)
    return lax.ppermute(values, axis, [(i, i ^ bit) for i in range(count)])


def swap_x(values):
    return swap(values, "mp", 1)


def swap_core(values):
    return swap(values, "dp", CORE)


def join(mine, other, upper):
    return jnp.concatenate([jnp.where(upper, other, mine), jnp.where(upper, mine, other)], axis=0)


def bit_of(index, bit):
    return (index & bit) != 0


def dot_f32(left, right, left_axis, right_axis):
    return lax.dot_general(
        left, right, (((left_axis,), (right_axis,)), ((), ())), preferred_element_type=jnp.float32
    )


def after(value, *held):
    return lax.optimization_barrier((value,) + held)[0]


def half_of(values, upper, half):
    return jnp.where(upper, values[half:], values[:half])


def pair_terms(scores, matched):
    decay = jnp.exp(-jnp.abs(scores))
    loss = jnp.maximum(scores, 0.0) + jnp.log1p(decay) - jnp.where(matched, scores, 0.0)
    ratio = 1.0 / (1.0 + decay)
    above = jnp.where((scores >= 0.0) != matched, ratio, decay * ratio)
    return loss, jnp.where(matched, -above, above)


def slice_plan(
    image_pooled,
    text_last,
    caption_of,
    image_gain,
    text_gain,
    mlp_up,
    mlp_down,
    adapter,
    logit_scale,
    logit_bias,
):
    rows = image_pooled.shape[0]
    half_rows = rows // 2
    quarter = rows // 4
    dp = lax.axis_index("dp")
    mp = lax.axis_index("mp")
    dp_count = lax.axis_size("dp")
    pair_count = rows * dp_count
    width = image_pooled.shape[1]
    own_c, own_y, own_z1, own_z2 = (bit_of(dp, b) for b in (CORE, Y, Z_LOW, Z_HIGH))
    own_x = bit_of(mp, 1)
    upper_of = {Y: own_y, Z_LOW: own_z1, Z_HIGH: own_z2}

    def grow(values, bit, *held):
        other = swap(values, "dp", bit)
        if held:
            other = after(other, *held)
        return join(values, other, upper_of[bit])

    parts = jnp.concatenate([caption_of // 128, caption_of % 128]).astype(jnp.bfloat16)
    extra = jnp.pad(parts[None, :], ((0, 7), (0, width - 2 * rows)))
    text_a = jnp.concatenate([text_last[:half_rows], extra], axis=0)
    text_b = text_last[half_rows:]
    image_pooled = after(image_pooled, text_a)
    text_a = grow(text_a, Z_HIGH)
    text_b = grow(text_b, Y)

    in_width = adapter.shape[0]
    in_half = in_width // 2
    piece = swap_x(half_of(adapter, own_c, in_half))

    image_norm = layer_norm(image_pooled, image_gain).astype(jnp.bfloat16)
    hidden = jax.nn.gelu(
        jnp.dot(image_norm, mlp_up, preferred_element_type=jnp.float32), approximate=True
    ).astype(jnp.bfloat16)
    branch = jnp.dot(hidden, mlp_down, preferred_element_type=jnp.float32)
    arrived = swap_x(half_of(branch, ~own_x, half_rows))
    feature = half_of(image_pooled, own_x, half_rows).astype(jnp.float32) + (
        half_of(branch, own_x, half_rows) + arrived
    )
    image_unit = (
        feature * lax.rsqrt(jnp.sum(feature * feature, axis=-1, keepdims=True) + EPS)
    ).astype(jnp.bfloat16)

    text_a = after(text_a, branch)
    text_b = after(text_b, branch)
    text_a = grow(text_a, Z_LOW)
    text_b = grow(text_b, Z_HIGH)
    other_adapter = join(piece, swap_core(piece), own_c)

    image_a = image_unit[:quarter]
    image_b = image_unit[quarter:]
    image_a = grow(image_a, Z_HIGH)
    image_b = join(image_b, swap_x(image_b), own_x)
    text_a = after(text_a, image_unit)
    text_b = after(text_b, image_unit)
    text_a = grow(text_a, Y)
    text_b = grow(text_b, Z_LOW)
    image_a = grow(image_a, Z_LOW)
    image_b = grow(image_b, Z_HIGH)
    image_a = grow(image_a, Y)
    image_b = grow(image_b, Z_LOW)
    far_a = swap_x(image_a)
    far_b = swap(image_b, "dp", Y)

    blocks = text_a.reshape(-1, half_rows + 8, width)
    parts = blocks[:, half_rows, : 2 * rows].astype(jnp.int32)
    captions = (parts[:, :rows] * 128 + parts[:, rows:]).reshape(2, 2, 2, 2, half_rows)
    cap_a = captions[:, :, :, 0].reshape(-1)
    cap_b = captions[:, :, :, 1].transpose(1, 2, 0, 3).reshape(-1)
    caption = jnp.concatenate([cap_a, cap_b])
    texts_raw = jnp.concatenate([blocks[:, :half_rows].reshape(-1, width), text_b], axis=0)

    text_norm = layer_norm(texts_raw, text_gain).astype(jnp.bfloat16)
    low, high = text_norm[:, :in_width], text_norm[:, in_width:]
    text_part = jnp.where(own_x, high, low)
    text_rest = jnp.where(own_x, low, high)
    texts = dot_f32(text_part, adapter, 1, 0) + dot_f32(text_rest, other_adapter, 1, 0)
    inverse = lax.rsqrt(jnp.sum(texts * texts, axis=-1, keepdims=True) + EPS)
    text_unit = texts * inverse
    text_embed = text_unit.astype(jnp.bfloat16)
    scale = logit_scale[0]
    shift = logit_bias[0]

    def places(bits):
        place = np.arange(quarter)
        for step in bits:
            place = np.concatenate([place, place + step])
        return place

    where_a = places((Z_HIGH * rows, Z_LOW * rows, Y * rows))
    where_b = places((half_rows, Z_HIGH * rows, Z_LOW * rows)) + quarter
    core_at = (dp & CORE) * rows
    y_at = (dp & Y) * rows
    x_at = mp * half_rows

    def score(images, place, offset):
        partner = swap_core(images)
        loss = 0.0
        weights = []
        for part, at in ((images, core_at), (partner, rows - core_at)):
            scores = scale * dot_f32(text_embed, part, 1, 1) + shift
            matched = (caption - (offset + at))[:, None] == place.astype(np.int32)[None, :]
            terms, weight = pair_terms(scores, matched)
            loss = loss + jnp.sum(terms)
            weights.append(weight.astype(jnp.bfloat16))
        return loss, dot_f32(jnp.concatenate(weights, 1), jnp.concatenate([images, partner]), 1, 0)

    loss_a, grads_a = score(image_a, where_a, x_at)
    loss_b, grads_b = score(image_b, where_b, y_at)
    loss_c, grads_c = score(far_a, where_a, half_rows - x_at)
    loss_d, grads_d = score(far_b, where_b, Y * rows - y_at)
    loss = (loss_a + loss_c) + (loss_b + loss_d)
    grads = (grads_a + grads_c) + (grads_b + grads_d)

    resid = text_resid(grads, text_unit, inverse, scale / pair_count)
    top = lax.reduce_precision(resid, 8, 7)
    rest = (resid - top).astype(jnp.bfloat16)
    top = top.astype(jnp.bfloat16)

    def outer(part):
        return dot_f32(part, top, 0, 0) + dot_f32(part, rest, 0, 0)

    first, second = text_part[:, :in_half], text_part[:, in_half:]
    given = outer(jnp.where(own_c, first, second))
    kept = outer(jnp.where(own_c, second, first))
    total = (kept + swap_core(given)).astype(jnp.bfloat16)
    grad_adapter = join(total, swap_core(total), own_c)
    loss = loss.reshape(1)
    mean_loss = (loss + swap_core(loss)) / (pair_count * pair_count)
    return grad_adapter, mean_loss


def solution(mesh):
    placed = (
        P("dp", None),
        P("dp", None),
        P("dp"),
        P(),
        P(),
        P(None, "mp"),
        P("mp", None),
        P("mp", None),
        P(),
        P(),
    )
    plan = slice_plan if dict(mesh.shape) == {"dp": 16, "mp": 2} else general_plan
    return jax.shard_map(
        plan, mesh=mesh, in_specs=placed, out_specs=(P("mp", None), P()), check_vma=False
    )
```

```python
import functools

import jax
import jax.numpy as jnp
import numpy as np
from jax import lax
from jax.experimental import pallas as pl
from jax.experimental.pallas import tpu as pltpu
from jax.sharding import PartitionSpec as P

EPS = 1e-06
CORE, Y, Z_LOW, Z_HIGH = 1, 2, 4, 8
CAPTION_BASE = 128
EXTRA = 8
BLOCK = 256
MIB = 1024 * 1024
SMEM = pl.BlockSpec(memory_space=pltpu.SMEM)


def layer_norm(values, gain):
    values = values.astype(jnp.float32)
    center = values - jnp.mean(values, axis=-1, keepdims=True)
    spread = jnp.mean(center * center, axis=-1, keepdims=True)
    return center * lax.rsqrt(spread + EPS) * gain


def text_resid(grads, text_unit, inverse, factor):
    scaled = grads * factor
    along = jnp.sum(text_unit * scaled, axis=-1, keepdims=True)
    return (scaled - text_unit * along) * inverse


def outer_sum(left, right):
    return lax.dot_general(
        left.astype(jnp.float32),
        right,
        (((0,), (0,)), ((), ())),
        precision=lax.Precision.HIGHEST,
        preferred_element_type=jnp.float32,
    )


def general_plan(
    image_pooled,
    text_last,
    caption_of,
    image_gain,
    text_gain,
    mlp_up,
    mlp_down,
    adapter,
    logit_scale,
    logit_bias,
):
    row_count = image_pooled.shape[0]
    mp_count = lax.axis_size("mp")
    mp_index = lax.axis_index("mp")
    dp_count = lax.axis_size("dp")
    half_rows = row_count // mp_count
    pair_count = row_count * dp_count
    image_norm = layer_norm(image_pooled, image_gain).astype(jnp.bfloat16)
    hidden = jax.nn.gelu(
        jnp.dot(image_norm, mlp_up, preferred_element_type=jnp.float32), approximate=True
    ).astype(jnp.bfloat16)
    branch = lax.psum_scatter(
        jnp.dot(hidden, mlp_down, preferred_element_type=jnp.float32),
        "mp",
        scatter_dimension=0,
        tiled=True,
    )
    own_pooled = lax.dynamic_slice_in_dim(image_pooled, mp_index * half_rows, half_rows, 0)
    feature = own_pooled.astype(jnp.float32) + branch
    image_unit = (
        feature * lax.rsqrt(jnp.sum(feature * feature, axis=-1, keepdims=True) + EPS)
    ).astype(jnp.bfloat16)
    text_norm = layer_norm(text_last, text_gain).astype(jnp.bfloat16)
    in_width = adapter.shape[0]
    text_part = lax.dynamic_slice_in_dim(text_norm, mp_index * in_width, in_width, 1)
    texts = lax.psum(jnp.dot(text_part, adapter, preferred_element_type=jnp.float32), "mp")
    inverse = lax.rsqrt(jnp.sum(texts * texts, axis=-1, keepdims=True) + EPS)
    text_unit = texts * inverse
    text_embed = text_unit.astype(jnp.bfloat16)
    scale = logit_scale[0]
    shift = logit_bias[0]
    piece = lax.all_gather(image_unit, "dp", axis=0, tiled=True)
    count = piece.shape[0]
    position = jnp.arange(count, dtype=jnp.int32)
    image_index = position // half_rows * row_count + mp_index * half_rows + position % half_rows
    logits = lax.dot_general(
        text_embed, piece, (((1,), (1,)), ((), ())), preferred_element_type=jnp.float32
    )
    labels = jnp.where(caption_of[:, None] == image_index[None, :], 1.0, -1.0).astype(jnp.float32)
    scores = scale * logits + shift
    loss_sum = jnp.sum(jax.nn.softplus(-labels * scores))
    pair_weight = (-labels * jax.nn.sigmoid(-labels * scores)).astype(jnp.bfloat16)
    grads = jnp.dot(pair_weight, piece, preferred_element_type=jnp.float32)
    grads, loss_sum = (grads, loss_sum)
    factor = scale / pair_count
    full_grads, loss_part = lax.psum((grads, loss_sum.reshape(1)), "mp")
    upper = outer_sum(text_part, text_resid(full_grads, text_unit, inverse, factor))
    grad_total, loss_total = lax.psum((upper, loss_part), "dp")
    mean_loss = loss_total / (pair_count * pair_count)
    return (grad_total.astype(jnp.bfloat16), mean_loss)


def swap(values, axis, bit):
    count = lax.axis_size(axis)
    return lax.ppermute(values, axis, [(i, i ^ bit) for i in range(count)])


def swap_x(values):
    return swap(values, "mp", 1)


def swap_core(values):
    return swap(values, "dp", CORE)


def join(mine, other, upper):
    return jnp.concatenate([jnp.where(upper, other, mine), jnp.where(upper, mine, other)], axis=0)


def bit_of(index, bit):
    return (index & bit) != 0


def after(value, *held):
    return lax.optimization_barrier((value,) + held)[0]


def half_of(values, upper, half):
    return jnp.where(upper, values[half:], values[:half])


def dot_f32(left, right, left_axis, right_axis):
    return lax.dot_general(
        left, right, (((left_axis,), (right_axis,)), ((), ())), preferred_element_type=jnp.float32
    )


def rows_spec(block, width):
    return pl.BlockSpec((block, width), lambda i: (i, 0))


def whole_spec(shape):
    return pl.BlockSpec(shape, lambda i: (0,) * len(shape))


def text_kernel(
    flags_ref, mine_a, other_a, mine_b, other_b, gain_ref, adapter_ref,
    embed_ref, unit_ref, inverse_ref, caption_ref, turned_ref, held,
):
    step = pl.program_id(0)
    rows = held.shape[1] - EXTRA
    for color, (mine, other) in enumerate(((mine_a, other_a), (mine_b, other_b))):
        upper = flags_ref[1 + color]

        @pl.when(step == 2 * color + upper)
        def _():
            held[...] = mine[...]

        @pl.when(step == 2 * color + 1 - upper)
        def _():
            held[...] = other[...]

    block = held[...]
    values = block[:, :rows].reshape(-1, block.shape[-1]).astype(jnp.float32)
    center = values - jnp.mean(values, axis=-1, keepdims=True)
    spread = jnp.mean(center * center, axis=-1, keepdims=True)
    normed = (center * lax.rsqrt(spread + EPS) * gain_ref[...]).astype(jnp.bfloat16)
    texts = jnp.dot(normed, adapter_ref[...], preferred_element_type=jnp.float32)
    inverse = lax.rsqrt(jnp.sum(texts * texts, axis=-1, keepdims=True) + EPS)
    unit = texts * inverse
    unit_ref[...] = unit
    inverse_ref[...] = inverse
    embed_ref[...] = unit.astype(jnp.bfloat16)
    row = lax.broadcasted_iota(jnp.int32, (rows, 2 * rows), 0)
    lane = lax.broadcasted_iota(jnp.int32, (rows, 2 * rows), 1)
    places = jnp.where(lane == row, float(CAPTION_BASE), jnp.where(lane == row + rows, 1.0, 0.0))
    for k in range(block.shape[0]):
        parts = block[k, rows : rows + EXTRA, : 2 * rows].astype(jnp.float32)[:1]
        number = jnp.sum(parts * places, axis=-1, keepdims=True)
        caption_ref[k * rows : (k + 1) * rows, :] = number.astype(jnp.int32)
    turned = normed.T
    half = turned.shape[0] // 2

    @pl.when(flags_ref[0] == 0)
    def _():
        turned_ref[...] = turned[:half]

    @pl.when(flags_ref[0] != 0)
    def _():
        turned_ref[...] = turned[half:]


def text_side(flags, pieces, gain, adapter):
    parts, padded, width = pieces[0].shape
    block = parts * (padded - EXTRA)
    count = 4 * block
    half = width // 2
    return pl.pallas_call(
        text_kernel,
        grid=(4,),
        in_specs=[SMEM]
        + [whole_spec(piece.shape) for piece in pieces]
        + [whole_spec((1, width)), whole_spec((width, width))],
        out_specs=[
            rows_spec(block, width),
            rows_spec(block, width),
            rows_spec(block, 1),
            rows_spec(block, 1),
            pl.BlockSpec((half, block), lambda i: (0, i)),
        ],
        out_shape=[
            jax.ShapeDtypeStruct((count, width), jnp.bfloat16),
            jax.ShapeDtypeStruct((count, width), jnp.float32),
            jax.ShapeDtypeStruct((count, 1), jnp.float32),
            jax.ShapeDtypeStruct((count, 1), jnp.int32),
            jax.ShapeDtypeStruct((half, count), jnp.bfloat16),
        ],
        scratch_shapes=[pltpu.VMEM(pieces[0].shape, jnp.bfloat16)],
        compiler_params=pltpu.CompilerParams(vmem_limit_bytes=40 * MIB),
        cost_estimate=pl.CostEstimate(
            flops=4 * count * width * width, bytes_accessed=10 * count * width, transcendentals=0
        ),
    )(flags, *pieces, gain.reshape(1, width), adapter)


def score_block(embed, caption, images, place, scale, shift):
    scores = scale * dot_f32(embed, images, 1, 1) + shift
    matched = caption == place
    decay = jnp.exp(-jnp.abs(scores))
    ratio = 1.0 / (1.0 + decay)
    weight = jnp.where((scores >= 0.0) != matched, ratio, decay * ratio)
    weight = jnp.where(matched, -weight, weight).astype(jnp.bfloat16)
    grads = jnp.dot(weight, images, preferred_element_type=jnp.float32)
    linear = jnp.maximum(scores, 0.0) - jnp.where(matched, scores, 0.0)
    grown = decay
    while grown.shape[0] > 16:
        half = grown.shape[0] // 2
        low, high = grown[:half], grown[half:]
        grown = low + high + low * high
    loss = jnp.sum(linear, axis=0, keepdims=True) + jnp.sum(jnp.log1p(grown), axis=0, keepdims=True)
    return grads, jnp.sum(loss, axis=1, keepdims=True)


def gather_parts(offsets_ref, parts, places, images, place):
    at = 0
    for k, (part, row) in enumerate(zip(parts, places)):
        count = part.shape[0]
        images[at : at + count, :] = part[...]
        place[:, at : at + count] = row[...] + offsets_ref[k]
        at += count


def early_kernel(parts, knobs_ref, offsets_ref, embed_ref, caption_ref, *refs):
    grads_ref, loss_ref, images, place = refs[2 * parts :]

    @pl.when(pl.program_id(0) == 0)
    def _():
        gather_parts(offsets_ref, refs[:parts], refs[parts : 2 * parts], images, place)
        loss_ref[...] = jnp.zeros_like(loss_ref)

    grads, loss = score_block(
        embed_ref[...], caption_ref[...], images[...], place[...], knobs_ref[0], knobs_ref[1]
    )
    grads_ref[...] = grads
    loss_ref[...] += jnp.broadcast_to(loss, loss_ref.shape)


def late_kernel(
    parts, knobs_ref, offsets_ref, embed_ref, caption_ref,
    early_ref, early_loss, unit_ref, inverse_ref, turned_ref, *refs,
):
    out_ref, images, place = refs[2 * parts :]
    half = turned_ref.shape[0]

    @pl.when(pl.program_id(0) == 0)
    def _():
        gather_parts(offsets_ref, refs[:parts], refs[parts : 2 * parts], images, place)
        out_ref[:half, :] = jnp.zeros((half, out_ref.shape[1]), jnp.float32)
        out_ref[half:, :] = jnp.broadcast_to(early_loss[0:1, 0:1], (EXTRA, out_ref.shape[1]))

    grads, loss = score_block(
        embed_ref[...], caption_ref[...], images[...], place[...], knobs_ref[0], knobs_ref[1]
    )
    unit = unit_ref[...]
    scaled = (grads + early_ref[...]) * knobs_ref[2]
    along = jnp.sum(unit * scaled, axis=-1, keepdims=True)
    resid = (scaled - unit * along) * inverse_ref[...]
    top = resid.astype(jnp.bfloat16)
    rest = (resid - top.astype(jnp.float32)).astype(jnp.bfloat16)
    turned = turned_ref[...]
    out_ref[:half, :] += jnp.dot(turned, top, preferred_element_type=jnp.float32) + jnp.dot(
        turned, rest, preferred_element_type=jnp.float32
    )
    out_ref[half:, :] += jnp.broadcast_to(loss, (EXTRA, out_ref.shape[1]))


def score_specs(embed, images, places):
    count, width = embed.shape
    total = sum(part.shape[0] for part in images)
    specs = [SMEM, SMEM, rows_spec(BLOCK, width), rows_spec(BLOCK, 1)]
    tail = [whole_spec(part.shape) for part in images] + [whole_spec(row.shape) for row in places]
    scratch = [pltpu.VMEM((total, width), jnp.bfloat16), pltpu.VMEM((1, total), jnp.int32)]
    return count, width, total, specs, tail, scratch


def early_scores(knobs, offsets, embed, caption, images, places):
    count, width, total, specs, tail, scratch = score_specs(embed, images, places)
    return pl.pallas_call(
        functools.partial(early_kernel, len(images)),
        grid=(count // BLOCK,),
        in_specs=specs + tail,
        out_specs=[rows_spec(BLOCK, width), whole_spec((8, 128))],
        out_shape=[
            jax.ShapeDtypeStruct((count, width), jnp.float32),
            jax.ShapeDtypeStruct((8, 128), jnp.float32),
        ],
        scratch_shapes=scratch,
        compiler_params=pltpu.CompilerParams(vmem_limit_bytes=40 * MIB),
        cost_estimate=pl.CostEstimate(
            flops=8 * count * width * total, bytes_accessed=8 * count * width, transcendentals=0
        ),
    )(knobs, offsets, embed, caption, *images, *places)


def late_scores(knobs, offsets, embed, caption, early, early_loss, unit, inverse, turned, images, places):
    count, width, total, specs, tail, scratch = score_specs(embed, images, places)
    half = turned.shape[0]
    return pl.pallas_call(
        functools.partial(late_kernel, len(images)),
        grid=(count // BLOCK,),
        in_specs=specs
        + [
            rows_spec(BLOCK, width),
            whole_spec((8, 128)),
            rows_spec(BLOCK, width),
            rows_spec(BLOCK, 1),
            pl.BlockSpec((half, BLOCK), lambda i: (0, i)),
        ]
        + tail,
        out_specs=whole_spec((half + EXTRA, width)),
        out_shape=jax.ShapeDtypeStruct((half + EXTRA, width), jnp.float32),
        scratch_shapes=scratch,
        compiler_params=pltpu.CompilerParams(vmem_limit_bytes=48 * MIB),
        cost_estimate=pl.CostEstimate(
            flops=8 * count * width * (total + half), bytes_accessed=16 * count * width, transcendentals=0
        ),
    )(knobs, offsets, embed, caption, early, early_loss, unit, inverse, turned, *images, *places)


def slice_plan(
    image_pooled,
    text_last,
    caption_of,
    image_gain,
    text_gain,
    mlp_up,
    mlp_down,
    adapter,
    logit_scale,
    logit_bias,
):
    rows, width = image_pooled.shape
    half_rows = rows // 2
    quarter = rows // 4
    dp = lax.axis_index("dp")
    mp = lax.axis_index("mp")
    pair_count = rows * lax.axis_size("dp")
    own_c = bit_of(dp, CORE)
    own_x = bit_of(mp, 1)

    def grow(values, bit):
        return join(values, swap(values, "dp", bit), bit_of(dp, bit))

    parts = jnp.stack([caption_of // CAPTION_BASE, caption_of % CAPTION_BASE]).astype(jnp.bfloat16)
    parts = parts.reshape(2, 2, half_rows).transpose(1, 0, 2).reshape(2, 1, rows)
    extra = jnp.pad(parts, ((0, 0), (0, EXTRA - 1), (0, width - rows)))
    packed = jnp.concatenate([text_last.reshape(2, half_rows, width), extra], axis=1)
    text_a, text_b = packed[:1], packed[1:]
    image_pooled = after(image_pooled, text_a, text_b)
    text_a = grow(text_a, Z_HIGH)
    text_b = grow(text_b, Y)

    in_half = adapter.shape[0] // 2
    piece = swap_x(half_of(adapter, own_c, in_half))

    image_norm = layer_norm(image_pooled, image_gain).astype(jnp.bfloat16)
    hidden = jax.nn.gelu(
        jnp.dot(image_norm, mlp_up, preferred_element_type=jnp.float32), approximate=True
    ).astype(jnp.bfloat16)
    branch = jnp.dot(hidden, mlp_down, preferred_element_type=jnp.float32)
    arrived = swap_x(half_of(branch, ~own_x, half_rows))
    feature = half_of(image_pooled, own_x, half_rows).astype(jnp.float32) + (
        half_of(branch, own_x, half_rows) + arrived
    )
    image_unit = (
        feature * lax.rsqrt(jnp.sum(feature * feature, axis=-1, keepdims=True) + EPS)
    ).astype(jnp.bfloat16)

    text_a = after(text_a, branch)
    text_b = after(text_b, branch)
    text_a = grow(text_a, Z_LOW)
    text_b = grow(text_b, Z_HIGH)
    other_adapter = join(piece, swap_core(piece), own_c)
    full_adapter = join(adapter, other_adapter, own_x)

    image_a = image_unit[:quarter]
    image_b = image_unit[quarter:]
    image_a = grow(image_a, Z_HIGH)
    image_b = join(image_b, swap_x(image_b), own_x)
    text_a = after(text_a, image_unit)
    text_b = after(text_b, image_unit)
    pieces = [text_a, swap(text_a, "dp", Y), text_b, swap(text_b, "dp", Z_LOW)]
    image_a = grow(image_a, Z_LOW)
    image_b = grow(image_b, Z_HIGH)
    image_a = grow(image_a, Y)
    image_b = grow(image_b, Z_LOW)
    far_a = swap_x(image_a)
    far_b = swap(image_b, "dp", Y)

    flags = jnp.stack([mp, (dp & Y) // Y, (dp & Z_LOW) // Z_LOW]).astype(jnp.int32)
    embed, unit, inverse, caption, turned = text_side(flags, pieces, text_gain, full_adapter)

    def places(bits):
        place = np.arange(quarter)
        for step in bits:
            place = np.concatenate([place, place + step])
        return place.astype(np.int32)[None, :]

    where_a = places((Z_HIGH * rows, Z_LOW * rows, Y * rows))
    where_b = places((half_rows, Z_HIGH * rows, Z_LOW * rows)) + quarter
    where = [where_a, where_a, where_b, where_b]
    core_at = (dp & CORE) * rows
    core_far = rows - core_at
    y_at = (dp & Y) * rows
    x_at = mp * half_rows
    x_far = half_rows - x_at
    y_far = Y * rows - y_at
    near = jnp.stack([x_at + core_at, x_at + core_far, y_at + core_at, y_at + core_far])
    far = jnp.stack([x_far + core_at, x_far + core_far, y_far + core_at, y_far + core_far])
    scale = logit_scale[0]
    knobs = jnp.stack([scale, logit_bias[0], scale / pair_count])

    images = [image_a, swap_core(image_a), image_b, swap_core(image_b)]
    early, early_loss = early_scores(knobs, near.astype(jnp.int32), embed, caption, images, where)
    images = [far_a, swap_core(far_a), far_b, swap_core(far_b)]
    part = late_scores(
        knobs, far.astype(jnp.int32), embed, caption, early, early_loss, unit, inverse, turned, images, where
    )
    total = part + swap_core(part)
    in_width = adapter.shape[0]
    mean_loss = total[in_width, :1] / (pair_count * pair_count)
    return total[:in_width].astype(jnp.bfloat16), mean_loss


def solution(mesh):
    placed = (
        P("dp", None),
        P("dp", None),
        P("dp"),
        P(),
        P(),
        P(None, "mp"),
        P("mp", None),
        P("mp", None),
        P(),
        P(),
    )
    plan = slice_plan if dict(mesh.shape) == {"dp": 16, "mp": 2} else general_plan
    return jax.shard_map(
        plan, mesh=mesh, in_specs=placed, out_specs=(P("mp", None), P()), check_vma=False
    )
```

```python
import functools

import jax
import jax.numpy as jnp
import numpy as np
from jax import lax
from jax.experimental import pallas as pl
from jax.experimental.pallas import tpu as pltpu
from jax.sharding import PartitionSpec as P

EPS = 1e-06
CORE, Y, Z_LOW, Z_HIGH = 1, 2, 4, 8
CAPTION_BASE = 128
EXTRA = 8
BLOCK = 256
VMEM_LIMIT = 40 * 1024 * 1024
SMEM = pl.BlockSpec(memory_space=pltpu.SMEM)


def layer_norm(values, gain):
    values = values.astype(jnp.float32)
    center = values - jnp.mean(values, axis=-1, keepdims=True)
    spread = jnp.mean(center * center, axis=-1, keepdims=True)
    return center * lax.rsqrt(spread + EPS) * gain


def text_resid(grads, text_unit, inverse, factor):
    scaled = grads * factor
    along = jnp.sum(text_unit * scaled, axis=-1, keepdims=True)
    return (scaled - text_unit * along) * inverse


def outer_sum(left, right):
    return lax.dot_general(
        left.astype(jnp.float32),
        right,
        (((0,), (0,)), ((), ())),
        precision=lax.Precision.HIGHEST,
        preferred_element_type=jnp.float32,
    )


def general_plan(
    image_pooled,
    text_last,
    caption_of,
    image_gain,
    text_gain,
    mlp_up,
    mlp_down,
    adapter,
    logit_scale,
    logit_bias,
):
    row_count = image_pooled.shape[0]
    mp_count = lax.axis_size("mp")
    mp_index = lax.axis_index("mp")
    dp_count = lax.axis_size("dp")
    half_rows = row_count // mp_count
    pair_count = row_count * dp_count
    image_norm = layer_norm(image_pooled, image_gain).astype(jnp.bfloat16)
    hidden = jax.nn.gelu(
        jnp.dot(image_norm, mlp_up, preferred_element_type=jnp.float32), approximate=True
    ).astype(jnp.bfloat16)
    branch = lax.psum_scatter(
        jnp.dot(hidden, mlp_down, preferred_element_type=jnp.float32),
        "mp",
        scatter_dimension=0,
        tiled=True,
    )
    own_pooled = lax.dynamic_slice_in_dim(image_pooled, mp_index * half_rows, half_rows, 0)
    feature = own_pooled.astype(jnp.float32) + branch
    image_unit = (
        feature * lax.rsqrt(jnp.sum(feature * feature, axis=-1, keepdims=True) + EPS)
    ).astype(jnp.bfloat16)
    text_norm = layer_norm(text_last, text_gain).astype(jnp.bfloat16)
    in_width = adapter.shape[0]
    text_part = lax.dynamic_slice_in_dim(text_norm, mp_index * in_width, in_width, 1)
    texts = lax.psum(jnp.dot(text_part, adapter, preferred_element_type=jnp.float32), "mp")
    inverse = lax.rsqrt(jnp.sum(texts * texts, axis=-1, keepdims=True) + EPS)
    text_unit = texts * inverse
    text_embed = text_unit.astype(jnp.bfloat16)
    scale = logit_scale[0]
    shift = logit_bias[0]
    piece = lax.all_gather(image_unit, "dp", axis=0, tiled=True)
    count = piece.shape[0]
    position = jnp.arange(count, dtype=jnp.int32)
    image_index = position // half_rows * row_count + mp_index * half_rows + position % half_rows
    logits = lax.dot_general(
        text_embed, piece, (((1,), (1,)), ((), ())), preferred_element_type=jnp.float32
    )
    labels = jnp.where(caption_of[:, None] == image_index[None, :], 1.0, -1.0).astype(jnp.float32)
    scores = scale * logits + shift
    loss_sum = jnp.sum(jax.nn.softplus(-labels * scores))
    pair_weight = (-labels * jax.nn.sigmoid(-labels * scores)).astype(jnp.bfloat16)
    grads = jnp.dot(pair_weight, piece, preferred_element_type=jnp.float32)
    grads, loss_sum = (grads, loss_sum)
    factor = scale / pair_count
    full_grads, loss_part = lax.psum((grads, loss_sum.reshape(1)), "mp")
    upper = outer_sum(text_part, text_resid(full_grads, text_unit, inverse, factor))
    grad_total, loss_total = lax.psum((upper, loss_part), "dp")
    mean_loss = loss_total / (pair_count * pair_count)
    return (grad_total.astype(jnp.bfloat16), mean_loss)


def swap(values, axis, bit):
    count = lax.axis_size(axis)
    return lax.ppermute(values, axis, [(i, i ^ bit) for i in range(count)])


def swap_x(values):
    return swap(values, "mp", 1)


def swap_core(values):
    return swap(values, "dp", CORE)


def join(mine, other, upper):
    return jnp.concatenate([jnp.where(upper, other, mine), jnp.where(upper, mine, other)], axis=0)


def bit_of(index, bit):
    return (index & bit) != 0


def after(value, *held):
    return lax.optimization_barrier((value,) + held)[0]


def half_of(values, upper, half):
    return jnp.where(upper, values[half:], values[:half])


def dot_f32(left, right, left_axis, right_axis):
    return lax.dot_general(
        left, right, (((left_axis,), (right_axis,)), ((), ())), preferred_element_type=jnp.float32
    )


def rows_spec(block, width):
    return pl.BlockSpec((block, width), lambda i: (i, 0))


def whole_spec(shape):
    return pl.BlockSpec(shape, lambda i: (0,) * len(shape))


def text_kernel(
    flags_ref, own_ref, near_0, near_1, far_0, far_1, gain_ref, adapter_ref,
    embed_ref, unit_ref, inverse_ref, caption_ref, turned_ref, held,
):
    step = pl.program_id(0)
    count = held.shape[0]
    rows = held.shape[1] - EXTRA
    own, other = 2 * flags_ref[1], 2 - 2 * flags_ref[1]
    for k in range(2):

        @pl.when(step == own + k)
        def _():
            held[...] = own_ref[k * count : (k + 1) * count]

    @pl.when(step == other + flags_ref[0])
    def _():
        held[0] = near_0[0]
        held[1] = near_1[0]

    @pl.when(step == other + 1 - flags_ref[0])
    def _():
        held[0] = far_0[0]
        held[1] = far_1[0]

    block = held[...]
    values = block[:, :rows].reshape(-1, block.shape[-1]).astype(jnp.float32)
    center = values - jnp.mean(values, axis=-1, keepdims=True)
    spread = jnp.mean(center * center, axis=-1, keepdims=True)
    normed = (center * lax.rsqrt(spread + EPS) * gain_ref[...]).astype(jnp.bfloat16)
    texts = jnp.dot(normed, adapter_ref[...], preferred_element_type=jnp.float32)
    inverse = lax.rsqrt(jnp.sum(texts * texts, axis=-1, keepdims=True) + EPS)
    unit = texts * inverse
    unit_ref[...] = unit
    inverse_ref[...] = inverse
    embed_ref[...] = unit.astype(jnp.bfloat16)
    row = lax.broadcasted_iota(jnp.int32, (rows, 2 * rows), 0)
    lane = lax.broadcasted_iota(jnp.int32, (rows, 2 * rows), 1)
    places = jnp.where(lane == row, float(CAPTION_BASE), jnp.where(lane == row + rows, 1.0, 0.0))
    for k in range(block.shape[0]):
        parts = block[k, rows : rows + EXTRA, : 2 * rows].astype(jnp.float32)[:1]
        number = jnp.sum(parts * places, axis=-1, keepdims=True)
        caption_ref[k * rows : (k + 1) * rows, :] = number.astype(jnp.int32)
    turned = normed.T
    half = turned.shape[0] // 2

    @pl.when(flags_ref[0] == 0)
    def _():
        turned_ref[...] = turned[:half]

    @pl.when(flags_ref[0] != 0)
    def _():
        turned_ref[...] = turned[half:]


def text_side(flags, pieces, gain, adapter):
    padded, width = pieces[1].shape[1:]
    parts = 2
    block = parts * (padded - EXTRA)
    count = 4 * block
    half = width // 2
    return pl.pallas_call(
        text_kernel,
        grid=(4,),
        in_specs=[SMEM]
        + [whole_spec(piece.shape) for piece in pieces]
        + [whole_spec((1, width)), whole_spec((width, width))],
        out_specs=[
            rows_spec(block, width),
            rows_spec(block, width),
            rows_spec(block, 1),
            rows_spec(block, 1),
            pl.BlockSpec((half, block), lambda i: (0, i)),
        ],
        out_shape=[
            jax.ShapeDtypeStruct((count, width), jnp.bfloat16),
            jax.ShapeDtypeStruct((count, width), jnp.float32),
            jax.ShapeDtypeStruct((count, 1), jnp.float32),
            jax.ShapeDtypeStruct((count, 1), jnp.int32),
            jax.ShapeDtypeStruct((half, count), jnp.bfloat16),
        ],
        scratch_shapes=[pltpu.VMEM((parts, padded, width), jnp.bfloat16)],
        compiler_params=pltpu.CompilerParams(vmem_limit_bytes=VMEM_LIMIT),
        cost_estimate=pl.CostEstimate(
            flops=4 * count * width * width, bytes_accessed=10 * count * width, transcendentals=0
        ),
    )(flags, *pieces, gain.reshape(1, width), adapter)


def score_block(embed, caption, images, place, scale, shift):
    scores = scale * dot_f32(embed, images, 1, 1) + shift
    matched = caption == place
    decay = jnp.exp(-jnp.abs(scores))
    ratio = 1.0 / (1.0 + decay)
    weight = jnp.where((scores >= 0.0) != matched, ratio, decay * ratio)
    weight = jnp.where(matched, -weight, weight).astype(jnp.bfloat16)
    grads = jnp.dot(weight, images, preferred_element_type=jnp.float32)
    linear = jnp.maximum(scores, 0.0) - jnp.where(matched, scores, 0.0)
    grown = decay
    while grown.shape[0] > 16:
        half = grown.shape[0] // 2
        low, high = grown[:half], grown[half:]
        grown = low + high + low * high
    loss = jnp.sum(linear, axis=0, keepdims=True) + jnp.sum(jnp.log1p(grown), axis=0, keepdims=True)
    return grads, jnp.sum(loss, axis=1, keepdims=True)


def gather_parts(offsets_ref, parts, places, images, place):
    at = 0
    for k, (part, row) in enumerate(zip(parts, places)):
        count = part.shape[0]
        images[at : at + count, :] = part[...]
        place[:, at : at + count] = row[...] + offsets_ref[k]
        at += count


def early_kernel(parts, knobs_ref, offsets_ref, embed_ref, caption_ref, *refs):
    grads_ref, loss_ref, images, place = refs[2 * parts :]

    @pl.when(pl.program_id(0) == 0)
    def _():
        gather_parts(offsets_ref, refs[:parts], refs[parts : 2 * parts], images, place)
        loss_ref[...] = jnp.zeros_like(loss_ref)

    grads, loss = score_block(
        embed_ref[...], caption_ref[...], images[...], place[...], knobs_ref[0], knobs_ref[1]
    )
    grads_ref[...] = grads
    loss_ref[...] += jnp.broadcast_to(loss, loss_ref.shape)


def late_kernel(
    parts, knobs_ref, offsets_ref, embed_ref, caption_ref,
    early_ref, early_loss, unit_ref, inverse_ref, turned_ref, *refs,
):
    out_ref, loss_ref, images, place = refs[2 * parts :]

    @pl.when(pl.program_id(0) == 0)
    def _():
        gather_parts(offsets_ref, refs[:parts], refs[parts : 2 * parts], images, place)
        out_ref[...] = jnp.zeros_like(out_ref)
        loss_ref[...] = early_loss[...]

    grads, loss = score_block(
        embed_ref[...], caption_ref[...], images[...], place[...], knobs_ref[0], knobs_ref[1]
    )
    unit = unit_ref[...]
    scaled = (grads + early_ref[...]) * knobs_ref[2]
    along = jnp.sum(unit * scaled, axis=-1, keepdims=True)
    resid = (scaled - unit * along) * inverse_ref[...]
    top = resid.astype(jnp.bfloat16)
    rest = (resid - top.astype(jnp.float32)).astype(jnp.bfloat16)
    turned = turned_ref[...]
    out_ref[...] += jnp.dot(turned, top, preferred_element_type=jnp.float32) + jnp.dot(
        turned, rest, preferred_element_type=jnp.float32
    )
    loss_ref[...] += jnp.broadcast_to(loss, loss_ref.shape)


def score_specs(embed, images, places):
    count, width = embed.shape
    total = sum(part.shape[0] for part in images)
    specs = [SMEM, SMEM, rows_spec(BLOCK, width), rows_spec(BLOCK, 1)]
    tail = [whole_spec(part.shape) for part in images] + [whole_spec(row.shape) for row in places]
    scratch = [pltpu.VMEM((total, width), jnp.bfloat16), pltpu.VMEM((1, total), jnp.int32)]
    return count, width, total, specs, tail, scratch


def early_scores(knobs, offsets, embed, caption, images, places):
    count, width, total, specs, tail, scratch = score_specs(embed, images, places)
    return pl.pallas_call(
        functools.partial(early_kernel, len(images)),
        grid=(count // BLOCK,),
        in_specs=specs + tail,
        out_specs=[rows_spec(BLOCK, width), whole_spec((8, 128))],
        out_shape=[
            jax.ShapeDtypeStruct((count, width), jnp.float32),
            jax.ShapeDtypeStruct((8, 128), jnp.float32),
        ],
        scratch_shapes=scratch,
        compiler_params=pltpu.CompilerParams(vmem_limit_bytes=VMEM_LIMIT),
        cost_estimate=pl.CostEstimate(
            flops=8 * count * width * total, bytes_accessed=8 * count * width, transcendentals=0
        ),
    )(knobs, offsets, embed, caption, *images, *places)


def late_scores(knobs, offsets, embed, caption, early, early_loss, unit, inverse, turned, images, places):
    count, width, total, specs, tail, scratch = score_specs(embed, images, places)
    half = turned.shape[0]
    return pl.pallas_call(
        functools.partial(late_kernel, len(images)),
        grid=(count // BLOCK,),
        in_specs=specs
        + [
            rows_spec(BLOCK, width),
            whole_spec((8, 128)),
            rows_spec(BLOCK, width),
            rows_spec(BLOCK, 1),
            pl.BlockSpec((half, BLOCK), lambda i: (0, i)),
        ]
        + tail,
        out_specs=[whole_spec((half, width)), whole_spec((8, 128))],
        out_shape=[
            jax.ShapeDtypeStruct((half, width), jnp.float32),
            jax.ShapeDtypeStruct((8, 128), jnp.float32),
        ],
        scratch_shapes=scratch,
        compiler_params=pltpu.CompilerParams(vmem_limit_bytes=VMEM_LIMIT),
        cost_estimate=pl.CostEstimate(
            flops=8 * count * width * (total + half), bytes_accessed=16 * count * width, transcendentals=0
        ),
    )(knobs, offsets, embed, caption, early, early_loss, unit, inverse, turned, *images, *places)


def slice_plan(
    image_pooled,
    text_last,
    caption_of,
    image_gain,
    text_gain,
    mlp_up,
    mlp_down,
    adapter,
    logit_scale,
    logit_bias,
):
    rows, width = image_pooled.shape
    half_rows = rows // 2
    quarter = rows // 4
    dp = lax.axis_index("dp")
    mp = lax.axis_index("mp")
    pair_count = rows * lax.axis_size("dp")
    own_c = bit_of(dp, CORE)
    own_x = bit_of(mp, 1)

    def grow(values, bit):
        return join(values, swap(values, "dp", bit), bit_of(dp, bit))

    parts = jnp.concatenate([caption_of // CAPTION_BASE, caption_of % CAPTION_BASE])
    extra = jnp.pad(parts.astype(jnp.bfloat16)[None, :], ((0, EXTRA - 1), (0, width - 2 * rows)))
    packed = jnp.concatenate([text_last, extra], axis=0)[None]
    in_half = adapter.shape[0] // 2
    in_part = in_half // 2
    sent = half_of(adapter, own_c, in_half)
    image_pooled = after(image_pooled, packed, sent)
    z_high, z_low = bit_of(dp, Z_HIGH), bit_of(dp, Z_LOW)
    from_low = swap(packed, "dp", Z_LOW)
    from_high = swap(packed, "dp", Z_HIGH)
    piece_0 = swap_x(sent[:in_part])

    image_norm = layer_norm(image_pooled, image_gain).astype(jnp.bfloat16)
    hidden = jax.nn.gelu(
        jnp.dot(image_norm, mlp_up, preferred_element_type=jnp.float32), approximate=True
    ).astype(jnp.bfloat16)
    branch = jnp.dot(hidden, mlp_down, preferred_element_type=jnp.float32)
    branch, from_low, from_high, piece_0 = lax.optimization_barrier((branch, from_low, from_high, piece_0))
    from_both = swap(from_high, "dp", Z_LOW)
    arrived = swap_x(half_of(branch, ~own_x, half_rows))
    feature = half_of(image_pooled, own_x, half_rows).astype(jnp.float32) + (
        half_of(branch, own_x, half_rows) + arrived
    )
    image_unit = (
        feature * lax.rsqrt(jnp.sum(feature * feature, axis=-1, keepdims=True) + EPS)
    ).astype(jnp.bfloat16)

    image_unit, from_both = lax.optimization_barrier((image_unit, from_both))
    texts = join(join(packed, from_low, z_low), join(from_high, from_both, z_low), z_high)
    given = half_of(texts, own_x, 2)

    image_a = image_unit[:quarter]
    image_b = image_unit[quarter:]
    near_0 = swap(given[:1], "dp", Y)
    piece_1 = swap_x(sent[in_part:])
    image_a = grow(image_a, Z_HIGH)
    image_b = join(image_b, swap_x(image_b), own_x)
    image_a, image_b, near_0, piece_1 = lax.optimization_barrier((image_a, image_b, near_0, piece_1))
    piece = jnp.concatenate([piece_0, piece_1])
    other_adapter = join(piece, swap_core(piece), own_c)
    full_adapter = join(adapter, other_adapter, own_x)
    near_1 = swap(given[1:], "dp", Y)
    far_0 = swap_x(near_0)
    image_a = grow(image_a, Z_LOW)
    image_b = grow(image_b, Z_HIGH)
    image_a, image_b, near_1, far_0 = lax.optimization_barrier((image_a, image_b, near_1, far_0))
    far_1 = swap_x(near_1)
    image_a = grow(image_a, Y)
    image_b = grow(image_b, Z_LOW)
    image_a, image_b, far_1, full_adapter = lax.optimization_barrier((image_a, image_b, far_1, full_adapter))
    far_a = swap_x(image_a)
    far_b = swap(image_b, "dp", Y)

    flags = jnp.stack([mp, (dp & Y) // Y]).astype(jnp.int32)
    pieces = [texts, near_0, near_1, far_0, far_1]
    embed, unit, inverse, caption, turned = text_side(flags, pieces, text_gain, full_adapter)

    def places(bits):
        place = np.arange(quarter)
        for step in bits:
            place = np.concatenate([place, place + step])
        return place.astype(np.int32)[None, :]

    where_a = places((Z_HIGH * rows, Z_LOW * rows, Y * rows))
    where_b = places((half_rows, Z_HIGH * rows, Z_LOW * rows)) + quarter
    where = [where_a, where_a, where_b, where_b]
    core_at = (dp & CORE) * rows
    core_far = rows - core_at
    y_at = (dp & Y) * rows
    x_at = mp * half_rows
    x_far = half_rows - x_at
    y_far = Y * rows - y_at
    near = jnp.stack([x_at + core_at, x_at + core_far, y_at + core_at, y_at + core_far])
    far = jnp.stack([x_far + core_at, x_far + core_far, y_far + core_at, y_far + core_far])
    scale = logit_scale[0]
    knobs = jnp.stack([scale, logit_bias[0], scale / pair_count])

    images = [image_a, swap_core(image_a), image_b, swap_core(image_b)]
    early, early_loss = early_scores(knobs, near.astype(jnp.int32), embed, caption, images, where)
    images = [far_a, swap_core(far_a), far_b, swap_core(far_b)]
    part, loss = late_scores(
        knobs, far.astype(jnp.int32), embed, caption, early, early_loss, unit, inverse, turned, images, where
    )
    grad_adapter = (part + swap_core(part)).astype(jnp.bfloat16)
    mean_loss = (loss + swap_core(loss))[0, :1] / (pair_count * pair_count)
    return grad_adapter, mean_loss


def solution(mesh):
    placed = (
        P("dp", None),
        P("dp", None),
        P("dp"),
        P(),
        P(),
        P(None, "mp"),
        P("mp", None),
        P("mp", None),
        P(),
        P(),
    )
    plan = slice_plan if dict(mesh.shape) == {"dp": 16, "mp": 2} else general_plan
    return jax.shard_map(
        plan, mesh=mesh, in_specs=placed, out_specs=(P("mp", None), P()), check_vma=False
    )
```

```python
import functools

import jax
import jax.numpy as jnp
import numpy as np
from jax import lax
from jax.experimental import pallas as pl
from jax.experimental.pallas import tpu as pltpu
from jax.sharding import PartitionSpec as P

EPS = 1e-06
CORE, Y, Z_LOW, Z_HIGH = 1, 2, 4, 8
CAPTION_BASE = 128
EXTRA = 8
BLOCK = 256
VMEM_LIMIT = 40 * 1024 * 1024
SMEM = pl.BlockSpec(memory_space=pltpu.SMEM)


def layer_norm(values, gain):
    values = values.astype(jnp.float32)
    center = values - jnp.mean(values, axis=-1, keepdims=True)
    spread = jnp.mean(center * center, axis=-1, keepdims=True)
    return center * lax.rsqrt(spread + EPS) * gain


def text_resid(grads, text_unit, inverse, factor):
    scaled = grads * factor
    along = jnp.sum(text_unit * scaled, axis=-1, keepdims=True)
    return (scaled - text_unit * along) * inverse


def outer_sum(left, right):
    return lax.dot_general(
        left.astype(jnp.float32),
        right,
        (((0,), (0,)), ((), ())),
        precision=lax.Precision.HIGHEST,
        preferred_element_type=jnp.float32,
    )


def general_plan(
    image_pooled,
    text_last,
    caption_of,
    image_gain,
    text_gain,
    mlp_up,
    mlp_down,
    adapter,
    logit_scale,
    logit_bias,
):
    row_count = image_pooled.shape[0]
    mp_count = lax.axis_size("mp")
    mp_index = lax.axis_index("mp")
    dp_count = lax.axis_size("dp")
    half_rows = row_count // mp_count
    pair_count = row_count * dp_count
    image_norm = layer_norm(image_pooled, image_gain).astype(jnp.bfloat16)
    hidden = jax.nn.gelu(
        jnp.dot(image_norm, mlp_up, preferred_element_type=jnp.float32), approximate=True
    ).astype(jnp.bfloat16)
    branch = lax.psum_scatter(
        jnp.dot(hidden, mlp_down, preferred_element_type=jnp.float32),
        "mp",
        scatter_dimension=0,
        tiled=True,
    )
    own_pooled = lax.dynamic_slice_in_dim(image_pooled, mp_index * half_rows, half_rows, 0)
    feature = own_pooled.astype(jnp.float32) + branch
    image_unit = (
        feature * lax.rsqrt(jnp.sum(feature * feature, axis=-1, keepdims=True) + EPS)
    ).astype(jnp.bfloat16)
    text_norm = layer_norm(text_last, text_gain).astype(jnp.bfloat16)
    in_width = adapter.shape[0]
    text_part = lax.dynamic_slice_in_dim(text_norm, mp_index * in_width, in_width, 1)
    texts = lax.psum(jnp.dot(text_part, adapter, preferred_element_type=jnp.float32), "mp")
    inverse = lax.rsqrt(jnp.sum(texts * texts, axis=-1, keepdims=True) + EPS)
    text_unit = texts * inverse
    text_embed = text_unit.astype(jnp.bfloat16)
    scale = logit_scale[0]
    shift = logit_bias[0]
    piece = lax.all_gather(image_unit, "dp", axis=0, tiled=True)
    count = piece.shape[0]
    position = jnp.arange(count, dtype=jnp.int32)
    image_index = position // half_rows * row_count + mp_index * half_rows + position % half_rows
    logits = lax.dot_general(
        text_embed, piece, (((1,), (1,)), ((), ())), preferred_element_type=jnp.float32
    )
    labels = jnp.where(caption_of[:, None] == image_index[None, :], 1.0, -1.0).astype(jnp.float32)
    scores = scale * logits + shift
    loss_sum = jnp.sum(jax.nn.softplus(-labels * scores))
    pair_weight = (-labels * jax.nn.sigmoid(-labels * scores)).astype(jnp.bfloat16)
    grads = jnp.dot(pair_weight, piece, preferred_element_type=jnp.float32)
    grads, loss_sum = (grads, loss_sum)
    factor = scale / pair_count
    full_grads, loss_part = lax.psum((grads, loss_sum.reshape(1)), "mp")
    upper = outer_sum(text_part, text_resid(full_grads, text_unit, inverse, factor))
    grad_total, loss_total = lax.psum((upper, loss_part), "dp")
    mean_loss = loss_total / (pair_count * pair_count)
    return (grad_total.astype(jnp.bfloat16), mean_loss)


def swap(values, axis, bit):
    count = lax.axis_size(axis)
    return lax.ppermute(values, axis, [(i, i ^ bit) for i in range(count)])


def swap_x(values):
    return swap(values, "mp", 1)


def swap_core(values):
    return swap(values, "dp", CORE)


def join(mine, other, upper):
    return jnp.concatenate([jnp.where(upper, other, mine), jnp.where(upper, mine, other)], axis=0)


def bit_of(index, bit):
    return (index & bit) != 0


def after(value, *held):
    return lax.optimization_barrier((value,) + held)[0]


def half_of(values, upper, half):
    return jnp.where(upper, values[half:], values[:half])


def dot_f32(left, right, left_axis, right_axis):
    return lax.dot_general(
        left, right, (((left_axis,), (right_axis,)), ((), ())), preferred_element_type=jnp.float32
    )


def rows_spec(block, width):
    return pl.BlockSpec((block, width), lambda i: (i, 0))


def whole_spec(shape):
    return pl.BlockSpec(shape, lambda i: (0,) * len(shape))


def text_kernel(flags_ref, *refs):
    pieces, (gain_ref, adapter_ref) = refs[:8], refs[8:10]
    embed_ref, unit_ref, inverse_ref, caption_ref, turned_ref, held = refs[10:]
    step = pl.program_id(0)
    rows = held.shape[1] - EXTRA
    for k in range(4):

        @pl.when(step == k)
        def _():
            held[0] = pieces[2 * k][...]
            held[1] = pieces[2 * k + 1][...]

    block = held[...]
    values = block[:, :rows].reshape(-1, block.shape[-1]).astype(jnp.float32)
    center = values - jnp.mean(values, axis=-1, keepdims=True)
    spread = jnp.mean(center * center, axis=-1, keepdims=True)
    normed = (center * lax.rsqrt(spread + EPS) * gain_ref[...]).astype(jnp.bfloat16)
    texts = jnp.dot(normed, adapter_ref[...], preferred_element_type=jnp.float32)
    inverse = lax.rsqrt(jnp.sum(texts * texts, axis=-1, keepdims=True) + EPS)
    unit = texts * inverse
    unit_ref[...] = unit
    inverse_ref[...] = inverse
    embed_ref[...] = unit.astype(jnp.bfloat16)
    row = lax.broadcasted_iota(jnp.int32, (rows, 2 * rows), 0)
    lane = lax.broadcasted_iota(jnp.int32, (rows, 2 * rows), 1)
    places = jnp.where(lane == row, float(CAPTION_BASE), jnp.where(lane == row + rows, 1.0, 0.0))
    for k in range(block.shape[0]):
        parts = block[k, rows : rows + EXTRA, : 2 * rows].astype(jnp.float32)[:1]
        number = jnp.sum(parts * places, axis=-1, keepdims=True)
        caption_ref[k * rows : (k + 1) * rows, :] = number.astype(jnp.int32)
    turned = normed.T
    half = turned.shape[0] // 2

    @pl.when(flags_ref[0] == 0)
    def _():
        turned_ref[...] = turned[:half]

    @pl.when(flags_ref[0] != 0)
    def _():
        turned_ref[...] = turned[half:]


def text_side(flags, pieces, gain, adapter):
    padded, width = pieces[0].shape
    parts = 2
    block = parts * (padded - EXTRA)
    count = 4 * block
    half = width // 2
    return pl.pallas_call(
        text_kernel,
        grid=(4,),
        in_specs=[SMEM]
        + [whole_spec(piece.shape) for piece in pieces]
        + [whole_spec((1, width)), whole_spec((width, width))],
        out_specs=[
            rows_spec(block, width),
            rows_spec(block, width),
            rows_spec(block, 1),
            rows_spec(block, 1),
            pl.BlockSpec((half, block), lambda i: (0, i)),
        ],
        out_shape=[
            pltpu.HBM((count, width), jnp.bfloat16),
            pltpu.HBM((count, width), jnp.float32),
            pltpu.HBM((count, 1), jnp.float32),
            pltpu.HBM((count, 1), jnp.int32),
            pltpu.HBM((half, count), jnp.bfloat16),
        ],
        scratch_shapes=[pltpu.VMEM((parts, padded, width), jnp.bfloat16)],
        compiler_params=pltpu.CompilerParams(vmem_limit_bytes=VMEM_LIMIT),
        cost_estimate=pl.CostEstimate(
            flops=4 * count * width * width, bytes_accessed=10 * count * width, transcendentals=0
        ),
    )(flags, *pieces, gain.reshape(1, width), adapter)


def score_block(embed, caption, images, place, scale, shift):
    scores = scale * dot_f32(embed, images, 1, 1) + shift
    matched = caption == place
    decay = jnp.exp(-jnp.abs(scores))
    ratio = 1.0 / (1.0 + decay)
    weight = jnp.where((scores >= 0.0) != matched, ratio, decay * ratio)
    weight = jnp.where(matched, -weight, weight).astype(jnp.bfloat16)
    grads = jnp.dot(weight, images, preferred_element_type=jnp.float32)
    linear = jnp.maximum(scores, 0.0) - jnp.where(matched, scores, 0.0)
    grown = decay
    while grown.shape[0] > 16:
        half = grown.shape[0] // 2
        low, high = grown[:half], grown[half:]
        grown = low + high + low * high
    loss = jnp.sum(linear, axis=0, keepdims=True) + jnp.sum(jnp.log1p(grown), axis=0, keepdims=True)
    return grads, jnp.sum(loss, axis=1, keepdims=True)


def gather_parts(offsets_ref, parts, places, images, place):
    at = 0
    for k, (part, row) in enumerate(zip(parts, places)):
        count = part.shape[0]
        images[at : at + count, :] = part[...]
        place[:, at : at + count] = row[...] + offsets_ref[k]
        at += count


def early_kernel(parts, knobs_ref, offsets_ref, embed_ref, caption_ref, *refs):
    grads_ref, loss_ref, images, place = refs[2 * parts :]

    @pl.when(pl.program_id(0) == 0)
    def _():
        gather_parts(offsets_ref, refs[:parts], refs[parts : 2 * parts], images, place)
        loss_ref[...] = jnp.zeros_like(loss_ref)

    grads, loss = score_block(
        embed_ref[...], caption_ref[...], images[...], place[...], knobs_ref[0], knobs_ref[1]
    )
    grads_ref[...] = grads
    loss_ref[...] += jnp.broadcast_to(loss, loss_ref.shape)


def late_kernel(
    parts, knobs_ref, offsets_ref, embed_ref, caption_ref,
    early_ref, early_loss, unit_ref, inverse_ref, turned_ref, *refs,
):
    out_ref, loss_ref, images, place = refs[2 * parts :]

    @pl.when(pl.program_id(0) == 0)
    def _():
        gather_parts(offsets_ref, refs[:parts], refs[parts : 2 * parts], images, place)
        out_ref[...] = jnp.zeros_like(out_ref)
        loss_ref[...] = early_loss[...]

    grads, loss = score_block(
        embed_ref[...], caption_ref[...], images[...], place[...], knobs_ref[0], knobs_ref[1]
    )
    unit = unit_ref[...]
    scaled = (grads + early_ref[...]) * knobs_ref[2]
    along = jnp.sum(unit * scaled, axis=-1, keepdims=True)
    resid = (scaled - unit * along) * inverse_ref[...]
    top = resid.astype(jnp.bfloat16)
    rest = (resid - top.astype(jnp.float32)).astype(jnp.bfloat16)
    turned = turned_ref[...]
    out_ref[...] += jnp.dot(turned, top, preferred_element_type=jnp.float32) + jnp.dot(
        turned, rest, preferred_element_type=jnp.float32
    )
    loss_ref[...] += jnp.broadcast_to(loss, loss_ref.shape)


def score_specs(embed, images, places):
    count, width = embed.shape
    total = sum(part.shape[0] for part in images)
    specs = [SMEM, SMEM, rows_spec(BLOCK, width), rows_spec(BLOCK, 1)]
    tail = [whole_spec(part.shape) for part in images] + [whole_spec(row.shape) for row in places]
    scratch = [pltpu.VMEM((total, width), jnp.bfloat16), pltpu.VMEM((1, total), jnp.int32)]
    return count, width, total, specs, tail, scratch


def in_hbm(values):
    return pltpu.with_memory_space_constraint(values, pltpu.HBM)


def early_scores(knobs, offsets, embed, caption, images, places):
    count, width, total, specs, tail, scratch = score_specs(embed, images, places)
    return pl.pallas_call(
        functools.partial(early_kernel, len(images)),
        grid=(count // BLOCK,),
        in_specs=specs + tail,
        out_specs=[rows_spec(BLOCK, width), whole_spec((8, 128))],
        out_shape=[
            pltpu.HBM((count, width), jnp.float32),
            pltpu.HBM((8, 128), jnp.float32),
        ],
        scratch_shapes=scratch,
        compiler_params=pltpu.CompilerParams(vmem_limit_bytes=VMEM_LIMIT),
        cost_estimate=pl.CostEstimate(
            flops=8 * count * width * total, bytes_accessed=8 * count * width, transcendentals=0
        ),
    )(knobs, offsets, in_hbm(embed), in_hbm(caption), *images, *places)


def late_scores(knobs, offsets, embed, caption, early, early_loss, unit, inverse, turned, images, places):
    count, width, total, specs, tail, scratch = score_specs(embed, images, places)
    half = turned.shape[0]
    return pl.pallas_call(
        functools.partial(late_kernel, len(images)),
        grid=(count // BLOCK,),
        in_specs=specs
        + [
            rows_spec(BLOCK, width),
            whole_spec((8, 128)),
            rows_spec(BLOCK, width),
            rows_spec(BLOCK, 1),
            pl.BlockSpec((half, BLOCK), lambda i: (0, i)),
        ]
        + tail,
        out_specs=[whole_spec((half, width)), whole_spec((8, 128))],
        out_shape=[
            jax.ShapeDtypeStruct((half, width), jnp.float32),
            jax.ShapeDtypeStruct((8, 128), jnp.float32),
        ],
        scratch_shapes=scratch,
        compiler_params=pltpu.CompilerParams(vmem_limit_bytes=VMEM_LIMIT),
        cost_estimate=pl.CostEstimate(
            flops=8 * count * width * (total + half), bytes_accessed=16 * count * width, transcendentals=0
        ),
    )(
        knobs, offsets, in_hbm(embed), in_hbm(caption), in_hbm(early), early_loss,
        in_hbm(unit), in_hbm(inverse), in_hbm(turned), *images, *places,
    )


def slice_plan(
    image_pooled,
    text_last,
    caption_of,
    image_gain,
    text_gain,
    mlp_up,
    mlp_down,
    adapter,
    logit_scale,
    logit_bias,
):
    rows, width = image_pooled.shape
    half_rows = rows // 2
    quarter = rows // 4
    dp = lax.axis_index("dp")
    mp = lax.axis_index("mp")
    pair_count = rows * lax.axis_size("dp")
    own_c = bit_of(dp, CORE)
    own_x = bit_of(mp, 1)

    def grow(values, bit):
        return join(values, swap(values, "dp", bit), bit_of(dp, bit))

    parts = jnp.concatenate([caption_of // CAPTION_BASE, caption_of % CAPTION_BASE])
    extra = jnp.pad(parts.astype(jnp.bfloat16)[None, :], ((0, EXTRA - 1), (0, width - 2 * rows)))
    packed = jnp.concatenate([text_last, extra], axis=0)
    in_half = adapter.shape[0] // 2
    sent = lax.dynamic_slice_in_dim(adapter, (dp & CORE) * in_half, in_half, 0)
    image_pooled = after(image_pooled, packed, sent)
    from_high = swap(packed, "dp", Z_HIGH)
    from_low = swap(packed, "dp", Z_LOW)
    piece = swap_x(sent)

    image_norm = layer_norm(image_pooled, image_gain).astype(jnp.bfloat16)
    hidden = jax.nn.gelu(
        jnp.dot(image_norm, mlp_up, preferred_element_type=jnp.float32), approximate=True
    ).astype(jnp.bfloat16)
    branch = jnp.dot(hidden, mlp_down, preferred_element_type=jnp.float32)
    branch, from_low, from_high, piece = lax.optimization_barrier((branch, from_low, from_high, piece))
    from_both = swap(from_high, "dp", Z_LOW)
    near_0 = swap(jnp.where(own_x, from_high, packed), "dp", Y)
    arrived = swap_x(half_of(branch, ~own_x, half_rows))
    feature = half_of(image_pooled, own_x, half_rows).astype(jnp.float32) + (
        half_of(branch, own_x, half_rows) + arrived
    )
    image_unit = (
        feature * lax.rsqrt(jnp.sum(feature * feature, axis=-1, keepdims=True) + EPS)
    ).astype(jnp.bfloat16)

    image_unit, from_both, near_0 = lax.optimization_barrier((image_unit, from_both, near_0))
    near_1 = swap(jnp.where(own_x, from_both, from_low), "dp", Y)
    far_0 = swap_x(near_0)
    other_adapter = join(piece, swap_core(piece), own_c)
    full_adapter = join(adapter, other_adapter, own_x)

    image_a = image_unit[:quarter]
    image_b = image_unit[quarter:]
    image_a = grow(image_a, Z_HIGH)
    image_b = join(image_b, swap_x(image_b), own_x)
    image_a, image_b, near_1, far_0 = lax.optimization_barrier((image_a, image_b, near_1, far_0))
    far_1 = swap_x(near_1)
    image_a = grow(image_a, Z_LOW)
    image_b = grow(image_b, Z_HIGH)
    image_a, image_b, far_1, full_adapter = lax.optimization_barrier((image_a, image_b, far_1, full_adapter))
    flags = mp.astype(jnp.int32).reshape(1)
    pieces = [packed, from_low, from_high, from_both, near_0, near_1, far_0, far_1]
    embed, unit, inverse, caption, turned = text_side(flags, pieces, text_gain, full_adapter)
    image_a = grow(image_a, Y)
    image_b = grow(image_b, Z_LOW)
    image_a, image_b, caption = lax.optimization_barrier((image_a, image_b, caption))
    far_a = swap_x(image_a)
    far_b = swap(image_b, "dp", Y)

    def places(bits):
        place = np.arange(quarter)
        for step in bits:
            place = np.concatenate([place, place + step])
        return place.astype(np.int32)[None, :]

    where_a = places((Z_HIGH * rows, Z_LOW * rows, Y * rows))
    where_b = places((half_rows, Z_HIGH * rows, Z_LOW * rows)) + quarter
    where = [where_a, where_a, where_b, where_b]
    core_at = (dp & CORE) * rows
    core_far = rows - core_at
    y_at = (dp & Y) * rows
    x_at = mp * half_rows
    x_far = half_rows - x_at
    y_far = Y * rows - y_at
    near = jnp.stack([x_at + core_at, x_at + core_far, y_at + core_at, y_at + core_far])
    far = jnp.stack([x_far + core_at, x_far + core_far, y_far + core_at, y_far + core_far])
    scale = logit_scale[0]
    knobs = jnp.stack([scale, logit_bias[0], scale / pair_count])

    images = [image_a, swap_core(image_a), image_b, swap_core(image_b)]
    early, early_loss = early_scores(knobs, near.astype(jnp.int32), embed, caption, images, where)
    far_a, far_b, early_loss = lax.optimization_barrier((far_a, far_b, early_loss))
    images = [far_a, swap_core(far_a), far_b, swap_core(far_b)]
    part, loss = late_scores(
        knobs, far.astype(jnp.int32), embed, caption, early, early_loss, unit, inverse, turned, images, where
    )
    grad_adapter = (part + swap_core(part)).astype(jnp.bfloat16)
    mean_loss = (loss + swap_core(loss))[0, :1] / (pair_count * pair_count)
    return grad_adapter, mean_loss


def solution(mesh):
    placed = (
        P("dp", None),
        P("dp", None),
        P("dp"),
        P(),
        P(),
        P(None, "mp"),
        P("mp", None),
        P("mp", None),
        P(),
        P(),
    )
    plan = slice_plan if dict(mesh.shape) == {"dp": 16, "mp": 2} else general_plan
    return jax.shard_map(
        plan, mesh=mesh, in_specs=placed, out_specs=(P("mp", None), P()), check_vma=False
    )
```

```python
import functools

import jax
import jax.numpy as jnp
import numpy as np
from jax import lax
from jax.experimental import pallas as pl
from jax.experimental.pallas import tpu as pltpu
from jax.sharding import PartitionSpec as P

EPS = 1e-06
CORE, Y, Z_LOW, Z_HIGH = 1, 2, 4, 8
CAPTION_BASE = 128
EXTRA = 8
BLOCK = 256
VMEM_LIMIT = 40 * 1024 * 1024
SMEM = pl.BlockSpec(memory_space=pltpu.SMEM)


def layer_norm(values, gain):
    values = values.astype(jnp.float32)
    center = values - jnp.mean(values, axis=-1, keepdims=True)
    spread = jnp.mean(center * center, axis=-1, keepdims=True)
    return center * lax.rsqrt(spread + EPS) * gain


def text_resid(grads, text_unit, inverse, factor):
    scaled = grads * factor
    along = jnp.sum(text_unit * scaled, axis=-1, keepdims=True)
    return (scaled - text_unit * along) * inverse


def outer_sum(left, right):
    return lax.dot_general(
        left.astype(jnp.float32),
        right,
        (((0,), (0,)), ((), ())),
        precision=lax.Precision.HIGHEST,
        preferred_element_type=jnp.float32,
    )


def general_plan(
    image_pooled,
    text_last,
    caption_of,
    image_gain,
    text_gain,
    mlp_up,
    mlp_down,
    adapter,
    logit_scale,
    logit_bias,
):
    row_count = image_pooled.shape[0]
    mp_count = lax.axis_size("mp")
    mp_index = lax.axis_index("mp")
    dp_count = lax.axis_size("dp")
    half_rows = row_count // mp_count
    pair_count = row_count * dp_count
    image_norm = layer_norm(image_pooled, image_gain).astype(jnp.bfloat16)
    hidden = jax.nn.gelu(
        jnp.dot(image_norm, mlp_up, preferred_element_type=jnp.float32), approximate=True
    ).astype(jnp.bfloat16)
    branch = lax.psum_scatter(
        jnp.dot(hidden, mlp_down, preferred_element_type=jnp.float32),
        "mp",
        scatter_dimension=0,
        tiled=True,
    )
    own_pooled = lax.dynamic_slice_in_dim(image_pooled, mp_index * half_rows, half_rows, 0)
    feature = own_pooled.astype(jnp.float32) + branch
    image_unit = (
        feature * lax.rsqrt(jnp.sum(feature * feature, axis=-1, keepdims=True) + EPS)
    ).astype(jnp.bfloat16)
    text_norm = layer_norm(text_last, text_gain).astype(jnp.bfloat16)
    in_width = adapter.shape[0]
    text_part = lax.dynamic_slice_in_dim(text_norm, mp_index * in_width, in_width, 1)
    texts = lax.psum(jnp.dot(text_part, adapter, preferred_element_type=jnp.float32), "mp")
    inverse = lax.rsqrt(jnp.sum(texts * texts, axis=-1, keepdims=True) + EPS)
    text_unit = texts * inverse
    text_embed = text_unit.astype(jnp.bfloat16)
    scale = logit_scale[0]
    shift = logit_bias[0]
    piece = lax.all_gather(image_unit, "dp", axis=0, tiled=True)
    count = piece.shape[0]
    position = jnp.arange(count, dtype=jnp.int32)
    image_index = position // half_rows * row_count + mp_index * half_rows + position % half_rows
    logits = lax.dot_general(
        text_embed, piece, (((1,), (1,)), ((), ())), preferred_element_type=jnp.float32
    )
    labels = jnp.where(caption_of[:, None] == image_index[None, :], 1.0, -1.0).astype(jnp.float32)
    scores = scale * logits + shift
    loss_sum = jnp.sum(jax.nn.softplus(-labels * scores))
    pair_weight = (-labels * jax.nn.sigmoid(-labels * scores)).astype(jnp.bfloat16)
    grads = jnp.dot(pair_weight, piece, preferred_element_type=jnp.float32)
    grads, loss_sum = (grads, loss_sum)
    factor = scale / pair_count
    full_grads, loss_part = lax.psum((grads, loss_sum.reshape(1)), "mp")
    upper = outer_sum(text_part, text_resid(full_grads, text_unit, inverse, factor))
    grad_total, loss_total = lax.psum((upper, loss_part), "dp")
    mean_loss = loss_total / (pair_count * pair_count)
    return (grad_total.astype(jnp.bfloat16), mean_loss)


def swap(values, axis, bit):
    count = lax.axis_size(axis)
    return lax.ppermute(values, axis, [(i, i ^ bit) for i in range(count)])


def swap_x(values):
    return swap(values, "mp", 1)


def swap_core(values):
    return swap(values, "dp", CORE)


def join(mine, other, upper):
    return jnp.concatenate([jnp.where(upper, other, mine), jnp.where(upper, mine, other)], axis=0)


def bit_of(index, bit):
    return (index & bit) != 0


def after(value, *held):
    return lax.optimization_barrier((value,) + held)[0]


def half_of(values, upper, half):
    return jnp.where(upper, values[half:], values[:half])


def dot_f32(left, right, left_axis, right_axis):
    return lax.dot_general(
        left, right, (((left_axis,), (right_axis,)), ((), ())), preferred_element_type=jnp.float32
    )


def rows_spec(block, width):
    return pl.BlockSpec((block, width), lambda i: (i, 0))


def whole_spec(shape):
    return pl.BlockSpec(shape, lambda i: (0,) * len(shape))


def text_kernel(flags_ref, *refs):
    pieces, (gain_ref, adapter_ref) = refs[:8], refs[8:10]
    embed_ref, unit_ref, inverse_ref, caption_ref, turned_ref, held = refs[10:]
    step = pl.program_id(0)
    rows = held.shape[1] - EXTRA
    for k in range(4):

        @pl.when(step == k)
        def _():
            held[0] = pieces[2 * k][...]
            held[1] = pieces[2 * k + 1][...]

    block = held[...]
    values = block[:, :rows].reshape(-1, block.shape[-1]).astype(jnp.float32)
    center = values - jnp.mean(values, axis=-1, keepdims=True)
    spread = jnp.mean(center * center, axis=-1, keepdims=True)
    normed = (center * lax.rsqrt(spread + EPS) * gain_ref[...]).astype(jnp.bfloat16)
    texts = jnp.dot(normed, adapter_ref[...], preferred_element_type=jnp.float32)
    inverse = lax.rsqrt(jnp.sum(texts * texts, axis=-1, keepdims=True) + EPS)
    unit = texts * inverse
    unit_ref[...] = unit
    inverse_ref[...] = inverse
    embed_ref[...] = unit.astype(jnp.bfloat16)
    row = lax.broadcasted_iota(jnp.int32, (rows, 2 * rows), 0)
    lane = lax.broadcasted_iota(jnp.int32, (rows, 2 * rows), 1)
    places = jnp.where(lane == row, float(CAPTION_BASE), jnp.where(lane == row + rows, 1.0, 0.0))
    for k in range(block.shape[0]):
        parts = block[k, rows : rows + EXTRA, : 2 * rows].astype(jnp.float32)[:1]
        number = jnp.sum(parts * places, axis=-1, keepdims=True)
        caption_ref[k * rows : (k + 1) * rows, :] = number.astype(jnp.int32)
    turned = normed.T
    half = turned.shape[0] // 2

    @pl.when(flags_ref[0] == 0)
    def _():
        turned_ref[...] = turned[:half]

    @pl.when(flags_ref[0] != 0)
    def _():
        turned_ref[...] = turned[half:]


def text_side(flags, pieces, gain, adapter):
    padded, width = pieces[0].shape
    parts = 2
    block = parts * (padded - EXTRA)
    count = 4 * block
    half = width // 2
    return pl.pallas_call(
        text_kernel,
        grid=(4,),
        in_specs=[SMEM]
        + [whole_spec(piece.shape) for piece in pieces]
        + [whole_spec((1, width)), whole_spec((width, width))],
        out_specs=[
            rows_spec(block, width),
            rows_spec(block, width),
            rows_spec(block, 1),
            rows_spec(block, 1),
            pl.BlockSpec((half, block), lambda i: (0, i)),
        ],
        out_shape=[
            pltpu.HBM((count, width), jnp.bfloat16),
            pltpu.HBM((count, width), jnp.float32),
            pltpu.HBM((count, 1), jnp.float32),
            pltpu.HBM((count, 1), jnp.int32),
            pltpu.HBM((half, count), jnp.bfloat16),
        ],
        scratch_shapes=[pltpu.VMEM((parts, padded, width), jnp.bfloat16)],
        compiler_params=pltpu.CompilerParams(vmem_limit_bytes=VMEM_LIMIT),
        cost_estimate=pl.CostEstimate(
            flops=4 * count * width * width, bytes_accessed=10 * count * width, transcendentals=0
        ),
    )(flags, *pieces, gain.reshape(1, width), adapter)


def score_block(embed, caption, images, place, scale, shift):
    scores = scale * dot_f32(embed, images, 1, 1) + shift
    matched = caption == place
    decay = jnp.exp(-jnp.abs(scores))
    ratio = 1.0 / (1.0 + decay)
    weight = jnp.where((scores >= 0.0) != matched, ratio, decay * ratio)
    weight = jnp.where(matched, -weight, weight).astype(jnp.bfloat16)
    grads = jnp.dot(weight, images, preferred_element_type=jnp.float32)
    linear = jnp.maximum(scores, 0.0) - jnp.where(matched, scores, 0.0)
    grown = decay
    while grown.shape[0] > 16:
        half = grown.shape[0] // 2
        low, high = grown[:half], grown[half:]
        grown = low + high + low * high
    loss = jnp.sum(linear, axis=0, keepdims=True) + jnp.sum(jnp.log1p(grown), axis=0, keepdims=True)
    return grads, jnp.sum(loss, axis=1, keepdims=True)


def gather_parts(offsets_ref, parts, places, images, place):
    at = 0
    for k, (part, row) in enumerate(zip(parts, places)):
        count = part.shape[0]
        images[at : at + count, :] = part[...]
        place[:, at : at + count] = row[...] + offsets_ref[k]
        at += count


def early_kernel(parts, knobs_ref, offsets_ref, embed_ref, caption_ref, *refs):
    grads_ref, loss_ref, images, place = refs[2 * parts :]

    @pl.when(pl.program_id(0) == 0)
    def _():
        gather_parts(offsets_ref, refs[:parts], refs[parts : 2 * parts], images, place)
        loss_ref[...] = jnp.zeros_like(loss_ref)

    grads, loss = score_block(
        embed_ref[...], caption_ref[...], images[...], place[...], knobs_ref[0], knobs_ref[1]
    )
    grads_ref[...] = grads
    loss_ref[...] += jnp.broadcast_to(loss, loss_ref.shape)


def late_kernel(
    parts, knobs_ref, offsets_ref, embed_ref, caption_ref,
    early_ref, early_loss, unit_ref, inverse_ref, turned_ref, *refs,
):
    out_ref, loss_ref, images, place = refs[2 * parts :]

    @pl.when(pl.program_id(0) == 0)
    def _():
        gather_parts(offsets_ref, refs[:parts], refs[parts : 2 * parts], images, place)
        out_ref[...] = jnp.zeros_like(out_ref)
        loss_ref[...] = early_loss[...]

    grads, loss = score_block(
        embed_ref[...], caption_ref[...], images[...], place[...], knobs_ref[0], knobs_ref[1]
    )
    unit = unit_ref[...]
    scaled = (grads + early_ref[...]) * knobs_ref[2]
    along = jnp.sum(unit * scaled, axis=-1, keepdims=True)
    resid = (scaled - unit * along) * inverse_ref[...]
    top = resid.astype(jnp.bfloat16)
    rest = (resid - top.astype(jnp.float32)).astype(jnp.bfloat16)
    turned = turned_ref[...]
    out_ref[...] += jnp.dot(turned, top, preferred_element_type=jnp.float32) + jnp.dot(
        turned, rest, preferred_element_type=jnp.float32
    )
    loss_ref[...] += jnp.broadcast_to(loss, loss_ref.shape)


def score_specs(embed, images, places):
    count, width = embed.shape
    total = sum(part.shape[0] for part in images)
    specs = [SMEM, SMEM, rows_spec(BLOCK, width), rows_spec(BLOCK, 1)]
    tail = [whole_spec(part.shape) for part in images] + [whole_spec(row.shape) for row in places]
    scratch = [pltpu.VMEM((total, width), jnp.bfloat16), pltpu.VMEM((1, total), jnp.int32)]
    return count, width, total, specs, tail, scratch


def in_hbm(values):
    return pltpu.with_memory_space_constraint(values, pltpu.HBM)


def early_scores(knobs, offsets, embed, caption, images, places):
    count, width, total, specs, tail, scratch = score_specs(embed, images, places)
    return pl.pallas_call(
        functools.partial(early_kernel, len(images)),
        grid=(count // BLOCK,),
        in_specs=specs + tail,
        out_specs=[rows_spec(BLOCK, width), whole_spec((8, 128))],
        out_shape=[
            pltpu.HBM((count, width), jnp.float32),
            pltpu.HBM((8, 128), jnp.float32),
        ],
        scratch_shapes=scratch,
        compiler_params=pltpu.CompilerParams(vmem_limit_bytes=VMEM_LIMIT),
        cost_estimate=pl.CostEstimate(
            flops=8 * count * width * total, bytes_accessed=8 * count * width, transcendentals=0
        ),
    )(knobs, offsets, in_hbm(embed), in_hbm(caption), *images, *places)


def late_scores(knobs, offsets, embed, caption, early, early_loss, unit, inverse, turned, images, places):
    count, width, total, specs, tail, scratch = score_specs(embed, images, places)
    half = turned.shape[0]
    return pl.pallas_call(
        functools.partial(late_kernel, len(images)),
        grid=(count // BLOCK,),
        in_specs=specs
        + [
            rows_spec(BLOCK, width),
            whole_spec((8, 128)),
            rows_spec(BLOCK, width),
            rows_spec(BLOCK, 1),
            pl.BlockSpec((half, BLOCK), lambda i: (0, i)),
        ]
        + tail,
        out_specs=[whole_spec((half, width)), whole_spec((8, 128))],
        out_shape=[
            jax.ShapeDtypeStruct((half, width), jnp.float32),
            jax.ShapeDtypeStruct((8, 128), jnp.float32),
        ],
        scratch_shapes=scratch,
        compiler_params=pltpu.CompilerParams(vmem_limit_bytes=VMEM_LIMIT),
        cost_estimate=pl.CostEstimate(
            flops=8 * count * width * (total + half), bytes_accessed=16 * count * width, transcendentals=0
        ),
    )(
        knobs, offsets, in_hbm(embed), in_hbm(caption), in_hbm(early), early_loss,
        in_hbm(unit), in_hbm(inverse), in_hbm(turned), *images, *places,
    )


def slice_plan(
    image_pooled,
    text_last,
    caption_of,
    image_gain,
    text_gain,
    mlp_up,
    mlp_down,
    adapter,
    logit_scale,
    logit_bias,
):
    rows, width = image_pooled.shape
    half_rows = rows // 2
    quarter = rows // 4
    dp = lax.axis_index("dp")
    mp = lax.axis_index("mp")
    pair_count = rows * lax.axis_size("dp")
    own_c = bit_of(dp, CORE)
    own_x = bit_of(mp, 1)

    def grow(values, bit):
        return join(values, swap(values, "dp", bit), bit_of(dp, bit))

    parts = jnp.concatenate([caption_of // CAPTION_BASE, caption_of % CAPTION_BASE])
    extra = jnp.pad(parts.astype(jnp.bfloat16)[None, :], ((0, EXTRA - 1), (0, width - 2 * rows)))
    packed = jnp.concatenate([text_last, extra], axis=0)
    in_half = adapter.shape[0] // 2
    sent = lax.dynamic_slice_in_dim(adapter, (dp & CORE) * in_half, in_half, 0)
    image_pooled = after(image_pooled, sent)
    piece = swap_x(sent)

    image_norm = layer_norm(image_pooled, image_gain).astype(jnp.bfloat16)
    image_norm, packed = lax.optimization_barrier((image_norm, packed))
    from_high = swap(packed, "dp", Z_HIGH)
    from_low = swap(packed, "dp", Z_LOW)
    hidden = jax.nn.gelu(
        jnp.dot(image_norm, mlp_up, preferred_element_type=jnp.float32), approximate=True
    ).astype(jnp.bfloat16)
    branch = jnp.dot(hidden, mlp_down, preferred_element_type=jnp.float32)
    branch, piece = lax.optimization_barrier((branch, piece))
    branch, from_low = lax.optimization_barrier((branch, from_low))
    from_both = swap(from_high, "dp", Z_LOW)
    near_0 = swap(jnp.where(own_x, from_high, packed), "dp", Y)
    arrived = swap_x(half_of(branch, ~own_x, half_rows))
    feature = half_of(image_pooled, own_x, half_rows).astype(jnp.float32) + (
        half_of(branch, own_x, half_rows) + arrived
    )
    image_unit = (
        feature * lax.rsqrt(jnp.sum(feature * feature, axis=-1, keepdims=True) + EPS)
    ).astype(jnp.bfloat16)

    image_unit, from_both, near_0 = lax.optimization_barrier((image_unit, from_both, near_0))
    near_1 = swap(jnp.where(own_x, from_both, from_low), "dp", Y)
    far_0 = swap_x(near_0)
    other_adapter = join(piece, swap_core(piece), own_c)
    full_adapter = join(adapter, other_adapter, own_x)

    image_a = image_unit[:quarter]
    image_b = image_unit[quarter:]
    image_a = grow(image_a, Z_HIGH)
    image_b = join(image_b, swap_x(image_b), own_x)
    image_a, image_b, near_1, far_0 = lax.optimization_barrier((image_a, image_b, near_1, far_0))
    far_1 = swap_x(near_1)
    image_a = grow(image_a, Z_LOW)
    image_b = grow(image_b, Z_HIGH)
    image_a, image_b, far_1, full_adapter = lax.optimization_barrier((image_a, image_b, far_1, full_adapter))
    flags = mp.astype(jnp.int32).reshape(1)
    pieces = [packed, from_low, from_high, from_both, near_0, near_1, far_0, far_1]
    embed, unit, inverse, caption, turned = text_side(flags, pieces, text_gain, full_adapter)
    image_a = grow(image_a, Y)
    image_b = grow(image_b, Z_LOW)
    image_a, image_b, caption = lax.optimization_barrier((image_a, image_b, caption))
    far_a = swap_x(image_a)
    far_b = swap(image_b, "dp", Y)

    def places(bits):
        place = np.arange(quarter)
        for step in bits:
            place = np.concatenate([place, place + step])
        return place.astype(np.int32)[None, :]

    where_a = places((Z_HIGH * rows, Z_LOW * rows, Y * rows))
    where_b = places((half_rows, Z_HIGH * rows, Z_LOW * rows)) + quarter
    where = [where_a, where_a, where_b, where_b]
    core_at = (dp & CORE) * rows
    core_far = rows - core_at
    y_at = (dp & Y) * rows
    x_at = mp * half_rows
    x_far = half_rows - x_at
    y_far = Y * rows - y_at
    near = jnp.stack([x_at + core_at, x_at + core_far, y_at + core_at, y_at + core_far])
    far = jnp.stack([x_far + core_at, x_far + core_far, y_far + core_at, y_far + core_far])
    scale = logit_scale[0]
    knobs = jnp.stack([scale, logit_bias[0], scale / pair_count])

    images = [image_a, swap_core(image_a), image_b, swap_core(image_b)]
    early, early_loss = early_scores(knobs, near.astype(jnp.int32), embed, caption, images, where)
    far_a, far_b, early_loss = lax.optimization_barrier((far_a, far_b, early_loss))
    images = [far_a, swap_core(far_a), far_b, swap_core(far_b)]
    part, loss = late_scores(
        knobs, far.astype(jnp.int32), embed, caption, early, early_loss, unit, inverse, turned, images, where
    )
    mean_loss = (loss + swap_core(loss))[0, :1] / (pair_count * pair_count)
    other, mean_loss = lax.optimization_barrier((swap_core(part), mean_loss))
    grad_adapter = (part + other).astype(jnp.bfloat16)
    return grad_adapter, mean_loss


def solution(mesh):
    placed = (
        P("dp", None),
        P("dp", None),
        P("dp"),
        P(),
        P(),
        P(None, "mp"),
        P("mp", None),
        P("mp", None),
        P(),
        P(),
    )
    plan = slice_plan if dict(mesh.shape) == {"dp": 16, "mp": 2} else general_plan
    return jax.shard_map(
        plan, mesh=mesh, in_specs=placed, out_specs=(P("mp", None), P()), check_vma=False
    )
```

```python
import functools

import jax
import jax.numpy as jnp
import numpy as np
from jax import lax
from jax.experimental import pallas as pl
from jax.experimental.pallas import tpu as pltpu
from jax.sharding import PartitionSpec as P

EPS = 1e-06
CORE, Y, Z_LOW, Z_HIGH = 1, 2, 4, 8
CAPTION_BASE = 128
EXTRA = 8
BLOCK = 256
VMEM_LIMIT = 40 * 1024 * 1024
SMEM = pl.BlockSpec(memory_space=pltpu.SMEM)


def layer_norm(values, gain):
    values = values.astype(jnp.float32)
    center = values - jnp.mean(values, axis=-1, keepdims=True)
    spread = jnp.mean(center * center, axis=-1, keepdims=True)
    return center * lax.rsqrt(spread + EPS) * gain


def text_resid(grads, text_unit, inverse, factor):
    scaled = grads * factor
    along = jnp.sum(text_unit * scaled, axis=-1, keepdims=True)
    return (scaled - text_unit * along) * inverse


def outer_sum(left, right):
    return lax.dot_general(
        left.astype(jnp.float32),
        right,
        (((0,), (0,)), ((), ())),
        precision=lax.Precision.HIGHEST,
        preferred_element_type=jnp.float32,
    )


def general_plan(
    image_pooled,
    text_last,
    caption_of,
    image_gain,
    text_gain,
    mlp_up,
    mlp_down,
    adapter,
    logit_scale,
    logit_bias,
):
    row_count = image_pooled.shape[0]
    mp_count = lax.axis_size("mp")
    mp_index = lax.axis_index("mp")
    dp_count = lax.axis_size("dp")
    half_rows = row_count // mp_count
    pair_count = row_count * dp_count
    image_norm = layer_norm(image_pooled, image_gain).astype(jnp.bfloat16)
    hidden = jax.nn.gelu(
        jnp.dot(image_norm, mlp_up, preferred_element_type=jnp.float32), approximate=True
    ).astype(jnp.bfloat16)
    branch = lax.psum_scatter(
        jnp.dot(hidden, mlp_down, preferred_element_type=jnp.float32),
        "mp",
        scatter_dimension=0,
        tiled=True,
    )
    own_pooled = lax.dynamic_slice_in_dim(image_pooled, mp_index * half_rows, half_rows, 0)
    feature = own_pooled.astype(jnp.float32) + branch
    image_unit = (
        feature * lax.rsqrt(jnp.sum(feature * feature, axis=-1, keepdims=True) + EPS)
    ).astype(jnp.bfloat16)
    text_norm = layer_norm(text_last, text_gain).astype(jnp.bfloat16)
    in_width = adapter.shape[0]
    text_part = lax.dynamic_slice_in_dim(text_norm, mp_index * in_width, in_width, 1)
    texts = lax.psum(jnp.dot(text_part, adapter, preferred_element_type=jnp.float32), "mp")
    inverse = lax.rsqrt(jnp.sum(texts * texts, axis=-1, keepdims=True) + EPS)
    text_unit = texts * inverse
    text_embed = text_unit.astype(jnp.bfloat16)
    scale = logit_scale[0]
    shift = logit_bias[0]
    piece = lax.all_gather(image_unit, "dp", axis=0, tiled=True)
    count = piece.shape[0]
    position = jnp.arange(count, dtype=jnp.int32)
    image_index = position // half_rows * row_count + mp_index * half_rows + position % half_rows
    logits = lax.dot_general(
        text_embed, piece, (((1,), (1,)), ((), ())), preferred_element_type=jnp.float32
    )
    labels = jnp.where(caption_of[:, None] == image_index[None, :], 1.0, -1.0).astype(jnp.float32)
    scores = scale * logits + shift
    loss_sum = jnp.sum(jax.nn.softplus(-labels * scores))
    pair_weight = (-labels * jax.nn.sigmoid(-labels * scores)).astype(jnp.bfloat16)
    grads = jnp.dot(pair_weight, piece, preferred_element_type=jnp.float32)
    grads, loss_sum = (grads, loss_sum)
    factor = scale / pair_count
    full_grads, loss_part = lax.psum((grads, loss_sum.reshape(1)), "mp")
    upper = outer_sum(text_part, text_resid(full_grads, text_unit, inverse, factor))
    grad_total, loss_total = lax.psum((upper, loss_part), "dp")
    mean_loss = loss_total / (pair_count * pair_count)
    return (grad_total.astype(jnp.bfloat16), mean_loss)


def swap(values, axis, bit):
    count = lax.axis_size(axis)
    return lax.ppermute(values, axis, [(i, i ^ bit) for i in range(count)])


def swap_x(values):
    return swap(values, "mp", 1)


def swap_core(values):
    return swap(values, "dp", CORE)


def join(mine, other, upper):
    return jnp.concatenate([jnp.where(upper, other, mine), jnp.where(upper, mine, other)], axis=0)


def bit_of(index, bit):
    return (index & bit) != 0


def after(value, *held):
    return lax.optimization_barrier((value,) + held)[0]


def half_of(values, upper, half):
    return jnp.where(upper, values[half:], values[:half])


def dot_f32(left, right, left_axis, right_axis):
    return lax.dot_general(
        left, right, (((left_axis,), (right_axis,)), ((), ())), preferred_element_type=jnp.float32
    )


def rows_spec(block, width):
    return pl.BlockSpec((block, width), lambda i: (i, 0))


def whole_spec(shape):
    return pl.BlockSpec(shape, lambda i: (0,) * len(shape))


def text_kernel(flags_ref, *refs):
    pieces, (gain_ref, adapter_ref) = refs[:8], refs[8:10]
    embed_ref, unit_ref, inverse_ref, caption_ref, turned_ref, held = refs[10:]
    step = pl.program_id(0)
    rows = held.shape[1] - EXTRA
    for k in range(4):

        @pl.when(step == k)
        def _():
            held[0] = pieces[2 * k][...]
            held[1] = pieces[2 * k + 1][...]

    block = held[...]
    values = block[:, :rows].reshape(-1, block.shape[-1]).astype(jnp.float32)
    center = values - jnp.mean(values, axis=-1, keepdims=True)
    spread = jnp.mean(center * center, axis=-1, keepdims=True)
    normed = (center * lax.rsqrt(spread + EPS) * gain_ref[...]).astype(jnp.bfloat16)
    texts = jnp.dot(normed, adapter_ref[...], preferred_element_type=jnp.float32)
    inverse = lax.rsqrt(jnp.sum(texts * texts, axis=-1, keepdims=True) + EPS)
    unit = texts * inverse
    unit_ref[...] = unit
    inverse_ref[...] = inverse
    embed_ref[...] = unit.astype(jnp.bfloat16)
    row = lax.broadcasted_iota(jnp.int32, (rows, 2 * rows), 0)
    lane = lax.broadcasted_iota(jnp.int32, (rows, 2 * rows), 1)
    places = jnp.where(lane == row, float(CAPTION_BASE), jnp.where(lane == row + rows, 1.0, 0.0))
    for k in range(block.shape[0]):
        parts = block[k, rows : rows + EXTRA, : 2 * rows].astype(jnp.float32)[:1]
        number = jnp.sum(parts * places, axis=-1, keepdims=True)
        caption_ref[k * rows : (k + 1) * rows, :] = number.astype(jnp.int32)
    turned = normed.T
    half = turned.shape[0] // 2

    @pl.when(flags_ref[0] == 0)
    def _():
        turned_ref[...] = turned[:half]

    @pl.when(flags_ref[0] != 0)
    def _():
        turned_ref[...] = turned[half:]


def text_side(flags, pieces, gain, adapter):
    padded, width = pieces[0].shape
    parts = 2
    block = parts * (padded - EXTRA)
    count = 4 * block
    half = width // 2
    return pl.pallas_call(
        text_kernel,
        grid=(4,),
        in_specs=[SMEM]
        + [whole_spec(piece.shape) for piece in pieces]
        + [whole_spec((1, width)), whole_spec((width, width))],
        out_specs=[
            rows_spec(block, width),
            rows_spec(block, width),
            rows_spec(block, 1),
            rows_spec(block, 1),
            pl.BlockSpec((half, block), lambda i: (0, i)),
        ],
        out_shape=[
            pltpu.HBM((count, width), jnp.bfloat16),
            pltpu.HBM((count, width), jnp.float32),
            pltpu.HBM((count, 1), jnp.float32),
            pltpu.HBM((count, 1), jnp.int32),
            pltpu.HBM((half, count), jnp.bfloat16),
        ],
        scratch_shapes=[pltpu.VMEM((parts, padded, width), jnp.bfloat16)],
        compiler_params=pltpu.CompilerParams(vmem_limit_bytes=VMEM_LIMIT),
        cost_estimate=pl.CostEstimate(
            flops=4 * count * width * width, bytes_accessed=10 * count * width, transcendentals=0
        ),
    )(flags, *pieces, gain.reshape(1, width), adapter)


def score_block(embed, caption, images, place, scale, shift):
    scores = scale * dot_f32(embed, images, 1, 1) + shift
    matched = caption == place
    decay = jnp.exp(-jnp.abs(scores))
    ratio = 1.0 / (1.0 + decay)
    weight = jnp.where((scores >= 0.0) != matched, ratio, decay * ratio)
    weight = jnp.where(matched, -weight, weight).astype(jnp.bfloat16)
    grads = jnp.dot(weight, images, preferred_element_type=jnp.float32)
    linear = jnp.maximum(scores, 0.0) - jnp.where(matched, scores, 0.0)
    grown = decay
    while grown.shape[0] > 16:
        half = grown.shape[0] // 2
        low, high = grown[:half], grown[half:]
        grown = low + high + low * high
    loss = jnp.sum(linear, axis=0, keepdims=True) + jnp.sum(jnp.log1p(grown), axis=0, keepdims=True)
    return grads, jnp.sum(loss, axis=1, keepdims=True)


def gather_parts(offsets_ref, parts, places, images, place):
    at = 0
    for k, (part, row) in enumerate(zip(parts, places)):
        count = part.shape[0]
        images[at : at + count, :] = part[...]
        place[:, at : at + count] = row[...] + offsets_ref[k]
        at += count


def early_kernel(parts, knobs_ref, offsets_ref, embed_ref, caption_ref, *refs):
    grads_ref, loss_ref, images, place = refs[2 * parts :]

    @pl.when(pl.program_id(0) == 0)
    def _():
        gather_parts(offsets_ref, refs[:parts], refs[parts : 2 * parts], images, place)
        loss_ref[...] = jnp.zeros_like(loss_ref)

    grads, loss = score_block(
        embed_ref[...], caption_ref[...], images[...], place[...], knobs_ref[0], knobs_ref[1]
    )
    grads_ref[...] = grads
    loss_ref[...] += jnp.broadcast_to(loss, loss_ref.shape)


def late_kernel(
    parts, knobs_ref, offsets_ref, embed_ref, caption_ref,
    early_ref, early_loss, unit_ref, inverse_ref, turned_ref, *refs,
):
    out_ref, loss_ref, images, place = refs[2 * parts :]

    @pl.when(pl.program_id(0) == 0)
    def _():
        gather_parts(offsets_ref, refs[:parts], refs[parts : 2 * parts], images, place)
        out_ref[...] = jnp.zeros_like(out_ref)
        loss_ref[...] = early_loss[...]

    grads, loss = score_block(
        embed_ref[...], caption_ref[...], images[...], place[...], knobs_ref[0], knobs_ref[1]
    )
    unit = unit_ref[...]
    scaled = (grads + early_ref[...]) * knobs_ref[2]
    along = jnp.sum(unit * scaled, axis=-1, keepdims=True)
    resid = (scaled - unit * along) * inverse_ref[...]
    top = resid.astype(jnp.bfloat16)
    rest = (resid - top.astype(jnp.float32)).astype(jnp.bfloat16)
    turned = turned_ref[...]
    out_ref[...] += jnp.dot(turned, top, preferred_element_type=jnp.float32) + jnp.dot(
        turned, rest, preferred_element_type=jnp.float32
    )
    loss_ref[...] += jnp.broadcast_to(loss, loss_ref.shape)


def score_specs(embed, images, places):
    count, width = embed.shape
    total = sum(part.shape[0] for part in images)
    specs = [SMEM, SMEM, rows_spec(BLOCK, width), rows_spec(BLOCK, 1)]
    tail = [whole_spec(part.shape) for part in images] + [whole_spec(row.shape) for row in places]
    scratch = [pltpu.VMEM((total, width), jnp.bfloat16), pltpu.VMEM((1, total), jnp.int32)]
    return count, width, total, specs, tail, scratch


def in_hbm(values):
    return pltpu.with_memory_space_constraint(values, pltpu.HBM)


def early_scores(knobs, offsets, embed, caption, images, places):
    count, width, total, specs, tail, scratch = score_specs(embed, images, places)
    return pl.pallas_call(
        functools.partial(early_kernel, len(images)),
        grid=(count // BLOCK,),
        in_specs=specs + tail,
        out_specs=[rows_spec(BLOCK, width), whole_spec((8, 128))],
        out_shape=[
            pltpu.HBM((count, width), jnp.float32),
            pltpu.HBM((8, 128), jnp.float32),
        ],
        scratch_shapes=scratch,
        compiler_params=pltpu.CompilerParams(vmem_limit_bytes=VMEM_LIMIT),
        cost_estimate=pl.CostEstimate(
            flops=8 * count * width * total, bytes_accessed=8 * count * width, transcendentals=0
        ),
    )(knobs, offsets, in_hbm(embed), in_hbm(caption), *images, *places)


def late_scores(knobs, offsets, embed, caption, early, early_loss, unit, inverse, turned, images, places):
    count, width, total, specs, tail, scratch = score_specs(embed, images, places)
    half = turned.shape[0]
    return pl.pallas_call(
        functools.partial(late_kernel, len(images)),
        grid=(count // BLOCK,),
        in_specs=specs
        + [
            rows_spec(BLOCK, width),
            whole_spec((8, 128)),
            rows_spec(BLOCK, width),
            rows_spec(BLOCK, 1),
            pl.BlockSpec((half, BLOCK), lambda i: (0, i)),
        ]
        + tail,
        out_specs=[whole_spec((half, width)), whole_spec((8, 128))],
        out_shape=[
            jax.ShapeDtypeStruct((half, width), jnp.float32),
            jax.ShapeDtypeStruct((8, 128), jnp.float32),
        ],
        scratch_shapes=scratch,
        compiler_params=pltpu.CompilerParams(vmem_limit_bytes=VMEM_LIMIT),
        cost_estimate=pl.CostEstimate(
            flops=8 * count * width * (total + half), bytes_accessed=16 * count * width, transcendentals=0
        ),
    )(
        knobs, offsets, in_hbm(embed), in_hbm(caption), in_hbm(early), early_loss,
        in_hbm(unit), in_hbm(inverse), in_hbm(turned), *images, *places,
    )


def slice_plan(
    image_pooled,
    text_last,
    caption_of,
    image_gain,
    text_gain,
    mlp_up,
    mlp_down,
    adapter,
    logit_scale,
    logit_bias,
):
    rows, width = image_pooled.shape
    half_rows = rows // 2
    quarter = rows // 4
    dp = lax.axis_index("dp")
    mp = lax.axis_index("mp")
    pair_count = rows * lax.axis_size("dp")
    own_c = bit_of(dp, CORE)
    own_x = bit_of(mp, 1)

    def grow(values, bit):
        return join(values, swap(values, "dp", bit), bit_of(dp, bit))

    parts = jnp.concatenate([caption_of // CAPTION_BASE, caption_of % CAPTION_BASE])
    extra = jnp.pad(parts.astype(jnp.bfloat16)[None, :], ((0, EXTRA - 1), (0, width - 2 * rows)))
    packed = jnp.concatenate([text_last, extra], axis=0)
    in_half = adapter.shape[0] // 2
    sent = lax.dynamic_slice_in_dim(adapter, (dp & CORE) * in_half, in_half, 0)
    image_pooled = after(image_pooled, sent)
    piece = swap_x(sent)

    image_norm = layer_norm(image_pooled, image_gain).astype(jnp.bfloat16)
    image_norm, packed = lax.optimization_barrier((image_norm, packed))
    from_high = swap(packed, "dp", Z_HIGH)
    from_low = swap(packed, "dp", Z_LOW)
    hidden = jax.nn.gelu(
        jnp.dot(image_norm, mlp_up, preferred_element_type=jnp.float32), approximate=True
    ).astype(jnp.bfloat16)
    branch = jnp.dot(hidden, mlp_down, preferred_element_type=jnp.float32)
    branch, piece = lax.optimization_barrier((branch, piece))
    from_both = swap(from_high, "dp", Z_LOW)
    near_0 = swap(jnp.where(own_x, from_high, packed), "dp", Y)
    arrived = swap_x(half_of(branch, ~own_x, half_rows))
    feature = half_of(image_pooled, own_x, half_rows).astype(jnp.float32) + (
        half_of(branch, own_x, half_rows) + arrived
    )
    image_unit = (
        feature * lax.rsqrt(jnp.sum(feature * feature, axis=-1, keepdims=True) + EPS)
    ).astype(jnp.bfloat16)

    image_unit, from_both, near_0, from_low = lax.optimization_barrier((image_unit, from_both, near_0, from_low))
    near_1 = swap(jnp.where(own_x, from_both, from_low), "dp", Y)
    far_0 = swap_x(near_0)
    other_adapter = join(piece, swap_core(piece), own_c)
    full_adapter = join(adapter, other_adapter, own_x)

    image_a = image_unit[:quarter]
    image_b = image_unit[quarter:]
    other_a = swap(image_a, "dp", Z_HIGH)
    other_b = swap_x(image_b)
    image_a, image_b, near_1, far_0 = lax.optimization_barrier((image_a, image_b, near_1, far_0))
    image_a = join(image_a, other_a, bit_of(dp, Z_HIGH))
    image_b = join(image_b, other_b, own_x)
    far_1 = swap_x(near_1)
    image_a = grow(image_a, Z_LOW)
    image_b = grow(image_b, Z_HIGH)
    image_a, image_b, far_1, full_adapter = lax.optimization_barrier((image_a, image_b, far_1, full_adapter))
    flags = mp.astype(jnp.int32).reshape(1)
    pieces = [packed, from_low, from_high, from_both, near_0, near_1, far_0, far_1]
    embed, unit, inverse, caption, turned = text_side(flags, pieces, text_gain, full_adapter)
    image_a = grow(image_a, Y)
    image_b = grow(image_b, Z_LOW)
    image_a, image_b, caption = lax.optimization_barrier((image_a, image_b, caption))
    far_a = swap_x(image_a)
    far_b = swap(image_b, "dp", Y)

    def places(bits):
        place = np.arange(quarter)
        for step in bits:
            place = np.concatenate([place, place + step])
        return place.astype(np.int32)[None, :]

    where_a = places((Z_HIGH * rows, Z_LOW * rows, Y * rows))
    where_b = places((half_rows, Z_HIGH * rows, Z_LOW * rows)) + quarter
    where = [where_a, where_a, where_b, where_b]
    core_at = (dp & CORE) * rows
    core_far = rows - core_at
    y_at = (dp & Y) * rows
    x_at = mp * half_rows
    x_far = half_rows - x_at
    y_far = Y * rows - y_at
    near = jnp.stack([x_at + core_at, x_at + core_far, y_at + core_at, y_at + core_far])
    far = jnp.stack([x_far + core_at, x_far + core_far, y_far + core_at, y_far + core_far])
    scale = logit_scale[0]
    knobs = jnp.stack([scale, logit_bias[0], scale / pair_count])

    images = [image_a, swap_core(image_a), image_b, swap_core(image_b)]
    early, early_loss = early_scores(knobs, near.astype(jnp.int32), embed, caption, images, where)
    far_a, far_b, early_loss = lax.optimization_barrier((far_a, far_b, early_loss))
    images = [far_a, swap_core(far_a), far_b, swap_core(far_b)]
    part, loss = late_scores(
        knobs, far.astype(jnp.int32), embed, caption, early, early_loss, unit, inverse, turned, images, where
    )
    mean_loss = (loss + swap_core(loss))[0, :1] / (pair_count * pair_count)
    other, mean_loss = lax.optimization_barrier((swap_core(part), mean_loss))
    grad_adapter = (part + other).astype(jnp.bfloat16)
    return grad_adapter, mean_loss


def solution(mesh):
    placed = (
        P("dp", None),
        P("dp", None),
        P("dp"),
        P(),
        P(),
        P(None, "mp"),
        P("mp", None),
        P("mp", None),
        P(),
        P(),
    )
    plan = slice_plan if dict(mesh.shape) == {"dp": 16, "mp": 2} else general_plan
    return jax.shard_map(
        plan, mesh=mesh, in_specs=placed, out_specs=(P("mp", None), P()), check_vma=False
    )
```
